512 devices in a mesh: stream: 32 (over z, core), span: 16 (over y, x).
Axes of the slice: x: 4, y: 4, z: 16, core: 2. Of those that a mesh axis runs over, the one named last changes fastest.
Arguments:
- rhs: bfloat16 [32, 64, 8, 32, 128], P('stream', 'span'), may hold values from -6 to 6
- previous: bfloat16 [32, 64, 8, 32, 128], P('stream', 'span'), may hold values from -6 to 6
- inverse_blocks: bfloat16 [32, 64, 8, 128, 128], P('stream', 'span'), as said below
- upstream_blocks: bfloat16 [32, 64, 8, 128, 128], P('stream', 'span'), may hold values from -1.1953125 to 1.1953125
- lower_gain: float32 [32, 64, 8, 128], P('stream', 'span'), may hold values from 0.2 to 1
- upper_gain: float32 [32, 64, 8, 128], P('stream', 'span'), may hold values from 0.2 to 1
- widths: int32 [32], P('stream'), may hold values from 2 to 8, as said below
- upstream_index: int32 [32, 64, 8], P('stream', 'span'), may hold values from 0 to 7, as said below
Outputs:
- swept: bfloat16 [32, 64, 8, 32, 128], P('stream', 'span')
The draws below stay inside these ranges and needn't reach their ends.
Inputs may be any that keep to these rules, and one draw needn't show every extreme that they name: `widths`: some section that has a following section has exactly 8 active clusters, and another has 2. `upstream_index`: for a section i after the first and an active slot k < widths[i], the entry is below widths[i - 1]; slot 0 of every slab names widths[i - 1] - 1. Entries of inactive slots and of the first section are 0. `inverse_blocks`: each block is the inverse of a diagonal block of the preconditioner, with entries of order 0.02 to 0.7 on its diagonal.
All inputs are finite; a program needn't handle non-finite values.
Results may differ from the reference program's by a relative error of at most 0.039.
Values may be sent and summed in bfloat16 or wider, within the bound.
No kernel may reach another device: no remote copies, remote signals or barrier semaphores. Data moves between devices by JAX's collectives and lax.ppermute only.
A program may use at most 64 MiB of HBM per device.

```python
import jax
import jax.numpy as jnp
from jax import lax

B = 128
NV = 32
KMAX = 8
SECTIONS = 32
SLABS = 64


def section_widths(key):
    key = jax.random.fold_in(key, 11)
    first_key, second_key, third_key = jax.random.split(key, 3)
    widths = jax.random.randint(first_key, (SECTIONS,), KMAX // 4, KMAX + 1)
    widest = jax.random.randint(second_key, (), 0, SECTIONS - 1)
    offset = jax.random.randint(third_key, (), 0, SECTIONS - 1)
    narrowest = (widest + 1 + offset) % SECTIONS
    places = jnp.arange(SECTIONS)
    widths = jnp.where(places == widest, KMAX, widths)
    widths = jnp.where(places == narrowest, KMAX // 4, widths)
    return widths.astype(jnp.int32)


def draw_widths(key, part):
    return section_widths(key)


def draw_upstream_index(key, part):
    widths = section_widths(key)
    key = jax.random.fold_in(key, 2)
    upstream = jnp.concatenate([jnp.ones((1,), jnp.int32), widths[:-1]])
    raw_values = jax.random.randint(key, (SECTIONS, SLABS, KMAX), 0, 1 << 20)
    chosen = raw_values % upstream[:, None, None]
    slots = jnp.arange(KMAX)[None, None, :]
    chosen = jnp.where(slots == 0, upstream[:, None, None] - 1, chosen)
    active = slots < widths[:, None, None]
    later = jnp.arange(SECTIONS)[:, None, None] > 0
    return jnp.where(active & later, chosen, 0).astype(jnp.int32)


def draw_inverse_blocks(key, part):
    key = jax.random.fold_in(key, 3)
    first_key, second_key = jax.random.split(key)
    shape = (SECTIONS, SLABS, KMAX, B, B)
    diagonal = jax.random.uniform(first_key, shape[:-1], jnp.float32, 0.5, 1.5)
    offdiag = jax.random.normal(second_key, shape, jnp.float32) * (0.5 * B ** (-0.5))
    identity = (jnp.arange(B)[:, None] == jnp.arange(B)[None, :]).astype(jnp.float32)
    blocks = 0.4 * (offdiag + identity * diagonal[..., :, None])
    return blocks.astype(jnp.bfloat16)


def steps_of(key, dims, cuts, smallest, high):
    loudness = 1.0
    for dim, shards_of in cuts:
        steps = jax.random.uniform(jax.random.fold_in(jax.random.fold_in(key, 6), dim), (shards_of,), jnp.float32, smallest / len(cuts), high / len(cuts))
        loudness = loudness * jnp.repeat(jnp.exp(steps), dims[dim] // shards_of).reshape((-1,) + (1,) * (len(dims) - 1 - dim))
    return loudness


def centred(stream_key, shape, deviation, reach, cuts=(), kind=jnp.bfloat16):
    array = deviation * jax.random.normal(stream_key, shape, jnp.float32)
    if cuts:
        array = array * steps_of(stream_key, shape, cuts, -0.22, 0.18)
    return jnp.clip(array, -reach, reach).astype(kind)


def setup_inputs(seed: int = 0) -> dict:
    key_list = jax.random.split(jax.random.key(seed), 9)
    return {
        "rhs": centred(key_list[0], (SECTIONS, SLABS, KMAX, NV, B), 1.0, 6.0, ((0, 32), (1, 16))),
        "previous": centred(key_list[1], (SECTIONS, SLABS, KMAX, NV, B), 1.0, 6.0, ((0, 32), (1, 16))),
        "inverse_blocks": draw_inverse_blocks(jax.random.fold_in(key_list[8], 71), 0),
        "upstream_blocks": centred(key_list[3], (SECTIONS, SLABS, KMAX, B, B), 0.185, 1.1953125, ((0, 32), (1, 16))),
        "lower_gain": jnp.clip(0.2 + 0.8 * jax.random.uniform(key_list[4], (SECTIONS, SLABS, KMAX, B), jnp.float32) ** steps_of(key_list[4], (SECTIONS, SLABS, KMAX, B), ((0, 32), (1, 16)), -0.2, 0.2), 0.2, 1.0),
        "upper_gain": jnp.clip(0.2 + 0.8 * jax.random.uniform(key_list[5], (SECTIONS, SLABS, KMAX, B), jnp.float32) ** steps_of(key_list[5], (SECTIONS, SLABS, KMAX, B), ((0, 32), (1, 16)), -0.2, 0.2), 0.2, 1.0),
        "widths": draw_widths(jax.random.fold_in(key_list[8], 71), 0),
        "upstream_index": draw_upstream_index(jax.random.fold_in(key_list[8], 71), 0),
    }


def reference(rhs, previous, inverse_blocks, upstream_blocks, lower_gain, upper_gain, widths, upstream_index):
    earlier = previous.astype(jnp.float32)
    empty_slab = jnp.zeros((SECTIONS, 1, KMAX, NV, B), jnp.float32)
    below_slab = jnp.concatenate([empty_slab, earlier[:, :-1]], axis=1)
    above_slab = jnp.concatenate([earlier[:, 1:], empty_slab], axis=1)
    side = lower_gain[:, :, :, None, :] * below_slab + upper_gain[:, :, :, None, :] * above_slab
    local_part = rhs.astype(jnp.float32) - side
    slots = jnp.arange(KMAX, dtype=jnp.int32)
    active_slots = slots[None, :] < widths[:, None]

    def advance(inflow, inputs):
        part_local, part_inverse, part_coupling, part_neighbour, part_active = inputs
        picked = jnp.take_along_axis(inflow, part_neighbour[:, :, None, None].astype(jnp.int32), axis=1)
        coupled = jnp.einsum("mkvj,mkij->mkvi", picked.astype(jnp.float32), part_coupling.astype(jnp.float32), precision=lax.Precision.HIGHEST)
        remainder = (part_local - coupled).astype(jnp.bfloat16)
        updated = jnp.einsum("mkvj,mkij->mkvi", remainder.astype(jnp.float32), part_inverse.astype(jnp.float32), precision=lax.Precision.HIGHEST).astype(jnp.bfloat16)
        updated = jnp.where(part_active[None, :, None, None], updated, jnp.zeros_like(updated))
        return updated, updated

    start = jnp.zeros((SLABS, KMAX, NV, B), jnp.bfloat16)
    last_value, swept = lax.scan(advance, start, (local_part, inverse_blocks, upstream_blocks, upstream_index, active_slots))
    return swept
```

```python
import functools

import jax
import jax.numpy as jnp
from jax import lax
from jax.experimental import pallas as pl
from jax.experimental.pallas import tpu as pltpu
from jax.sharding import PartitionSpec as P

F32 = jnp.float32
BF16 = jnp.bfloat16
SMEM = pl.BlockSpec(memory_space=pltpu.SMEM)
VMEM = pl.BlockSpec(memory_space=pltpu.VMEM)
ANY = pl.BlockSpec(memory_space=pl.ANY)
PAD = 16


def pin(x):
    return pltpu.with_memory_space_constraint(x, pltpu.VMEM)


def in_vmem(shape, dtype=BF16):
    return pltpu.VMEM(shape, dtype)


def params(mib=16):
    return pltpu.CompilerParams(vmem_limit_bytes=mib * 1024 * 1024)


def cost(flops, size):
    return pl.CostEstimate(flops=flops, bytes_accessed=size, transcendentals=0)


def dot(a, b, dims=((1,), (0,))):
    return lax.dot_general(a, b, (dims, ((), ())), preferred_element_type=F32)


def blocks_kernel(where, index, u_hbm, d_hbm, keep, send, u, d, u_sem, d_sem):
    core, width = where[0], where[1]
    slabs, slots, nb, _ = u.shape
    nv = (keep.shape[1] - PAD) // slots - nb
    copies = []
    for m in range(slabs):
        a = pltpu.make_async_copy(u_hbm.at[0, m], u.at[m], u_sem.at[m])
        b = pltpu.make_async_copy(d_hbm.at[0, m], d.at[m], d_sem.at[m])
        a.start()
        b.start()
        copies.append((a, b))
    for a, b in copies:
        a.wait()
        b.wait()
    half = slabs // 2
    rows = lax.broadcasted_iota(jnp.int32, (PAD, nb), 0)

    def body(j, _):
        for out, first in ((send, (1 - core) * half), (keep, core * half)):
            m = first + j
            tile = jnp.zeros((PAD, nb), F32)
            for k in range(slots):
                b = -dot(u[m, k], d[m, k], ((0,), (1,)))
                b = jnp.where(k < width, b, 0.0)
                out[j, pl.ds(k * (nv + nb) + nv, nb), :] = b.astype(BF16)
                tile = tile + jnp.where(rows == k, index[0, m, k].astype(F32), 0.0)
            out[j, pl.ds(slots * (nv + nb), PAD), :] = tile.astype(BF16)
        return 0

    lax.fori_loop(0, half, body, 0)


def vectors_kernel(where, rhs_hbm, prev_hbm, below, above, lower_hbm, upper_hbm, d_hbm, keep_in, send_in, keep, send,
                   rhs, prev, lower, upper, d, sem):
    core, width = where[0], where[1]
    slabs, slots, nv, nb = rhs.shape
    half = slabs // 2
    copies = [
        pltpu.make_async_copy(rhs_hbm.at[0], rhs, sem.at[0]),
        pltpu.make_async_copy(prev_hbm.at[0], prev.at[pl.ds(1, slabs)], sem.at[1]),
        pltpu.make_async_copy(lower_hbm.at[0], lower, sem.at[2]),
        pltpu.make_async_copy(upper_hbm.at[0], upper, sem.at[3]),
        pltpu.make_async_copy(d_hbm.at[0], d, sem.at[4]),
    ]
    for c in copies:
        c.start()
    prev[0] = below[0]
    prev[slabs + 1] = above[0]
    for c in copies:
        c.wait()

    def body(j, _):
        for out, first in ((send, (1 - core) * half), (keep, core * half)):
            m = first + j
            lo, up = lower[m], upper[m]
            for k in range(slots):
                side = lo[k : k + 1, :] * prev[m, k].astype(F32) + up[k : k + 1, :] * prev[m + 2, k].astype(F32)
                local = (rhs[m, k].astype(F32) - side).astype(BF16)
                c = dot(local, d[m, k], ((1,), (1,)))
                c = jnp.where(k < width, c, 0.0)
                out[j, pl.ds(k * (nv + nb), nv), :] = c.astype(BF16)
        return 0

    lax.fori_loop(0, half, body, 0)


def slot_scalars(tile, scratch, slots):
    scratch[...] = tile.astype(jnp.int32)
    return [scratch[k, 0] for k in range(slots)]


def compose(lo, hi, out, scratch, slots, nv, nb):
    step = nv + nb
    tile_lo = lo[pl.ds(slots * step, PAD), :].astype(F32)
    tile_hi = hi[pl.ds(slots * step, PAD), :].astype(F32)
    picks = slot_scalars(tile_hi, scratch, slots)
    tile = jnp.zeros_like(tile_hi)
    for n in range(slots):
        tile = tile + jnp.where(tile_hi == n, tile_lo[n : n + 1, :], 0.0)
    out[pl.ds(slots * step, PAD), :] = tile.astype(BF16)
    for k in range(slots):
        x = lo[pl.ds(pl.multiple_of(picks[k] * step, 16), step), :]
        y = dot(x, hi[pl.ds(k * step + nv, nb), :])
        c = hi[pl.ds(k * step, nv), :].astype(F32)
        out[pl.ds(k * step, nv), :] = (y[:nv] + c).astype(BF16)
        out[pl.ds(k * step + nv, nb), :] = y[nv:].astype(BF16)


def pair_kernel(slots, nv, where, keep, recv, out_keep, out_send, scratch):
    core, chip = where[0], where[2]
    for here, lo, hi in ((0, keep, recv), (1, recv, keep)):
        @pl.when(core == here)
        def _():
            compose(lo.at[1 - chip], hi.at[1 - chip], out_send, scratch, slots, nv, lo.shape[-1])
            compose(lo.at[chip], hi.at[chip], out_keep, scratch, slots, nv, lo.shape[-1])


def group_kernel(slots, nv, where, keep, recv, out, start, scratch):
    chip = where[2]
    nb = out.shape[-1]
    for here, lo, hi in ((0, keep, recv), (1, recv, keep)):
        @pl.when(chip == here)
        def _():
            compose(lo, hi, out, scratch, slots, nv, nb)
    for k in range(slots):
        start[k] = out[pl.ds(k * (nv + nb), nv), :]


def apply_map(x, m, out, scratch, slots, nv, nb):
    step = nv + nb
    picks = slot_scalars(m[pl.ds(slots * step, PAD), :].astype(F32), scratch, slots)
    for k in range(slots):
        y = dot(x[picks[k]], m[pl.ds(k * step + nv, nb), :])
        out[k] = (y + m[pl.ds(k * step, nv), :].astype(F32)).astype(BF16)


def hop_kernel(slots, nv, recv, group, inflow, out, inflow_out, scratch):
    apply_map(recv, group, out, scratch, slots, nv, group.shape[-1])
    inflow_out[...] = inflow[...] + recv[...]


def share_kernel(slots, nv, where, inflow, keep, recv, group, out, scratch):
    chip = where[2]
    nb = group.shape[-1]
    out[0] = inflow[...]
    for here, lo in ((0, keep), (1, recv)):
        @pl.when(chip == here)
        def _():
            apply_map(inflow, lo, out.at[1], scratch, slots, nv, nb)
    apply_map(inflow, group, out.at[2], scratch, slots, nv, nb)


def finish_kernel(slots, nv, where, index, shared, keep, send, out):
    core, chip = where[0], where[2]
    slabs = out.shape[1]
    half = slabs // 2
    nb = out.shape[-1]
    step = nv + nb
    for m in range(slabs):
        owner = 2 * (m % 2) + m // 2

        @pl.when(core == 1)
        def _():
            out[0, m] = shared[owner, 1 + chip]

        @pl.when(core == 0)
        def _():
            maps = keep if m < half else send
            for k in range(slots):
                x = shared[owner, chip, index[0, m, k]]
                y = dot(x, maps[m % half, pl.ds(k * step + nv, nb), :])
                out[0, m, k] = (y + maps[m % half, pl.ds(k * step, nv), :].astype(F32)).astype(BF16)


def local(rhs, previous, inverse_blocks, upstream_blocks, lower_gain, upper_gain, widths, upstream_index):
    _, slabs, slots, nv, nb = rhs.shape
    half = slabs // 2
    sections, peers = lax.axis_size("stream"), lax.axis_size("span")
    groups = sections // 4
    rows = slots * (nv + nb) + PAD
    position = lax.axis_index("stream")
    where = jnp.stack([position % 2, widths[0], (position // 2) % 2]).astype(jnp.int32)

    up = [(i, i + 1) for i in range(peers - 1)]
    down = [(j, i) for i, j in up]
    below = lax.ppermute(previous[0, slabs - 1 :], "span", up)
    above = lax.ppermute(previous[0, :1], "span", down)

    pair_shape = in_vmem((half, rows, nb))
    one_shape = in_vmem((rows, nb))
    vec_shape = in_vmem((slots, nv, nb))
    index_scratch = pltpu.VMEM((PAD, nb), jnp.int32)

    keep, send = pl.pallas_call(
        blocks_kernel,
        out_shape=(pair_shape, pair_shape),
        in_specs=[SMEM, SMEM, ANY, ANY],
        out_specs=(VMEM, VMEM),
        scratch_shapes=[
            pltpu.VMEM((slabs, slots, nb, nb), BF16),
            pltpu.VMEM((slabs, slots, nb, nb), BF16),
            pltpu.SemaphoreType.DMA((slabs,)),
            pltpu.SemaphoreType.DMA((slabs,)),
        ],
        compiler_params=params(),
        cost_estimate=cost(2 * slabs * slots * nb**3, 4 * slabs * slots * nb * nb),
        name="section_blocks",
    )(where, upstream_index, upstream_blocks, inverse_blocks)
    keep, send = pl.pallas_call(
        vectors_kernel,
        out_shape=(pair_shape, pair_shape),
        in_specs=[SMEM, ANY, ANY, VMEM, VMEM, ANY, ANY, ANY, VMEM, VMEM],
        out_specs=(VMEM, VMEM),
        scratch_shapes=[
            pltpu.VMEM((slabs, slots, nv, nb), BF16),
            pltpu.VMEM((slabs + 2, slots, nv, nb), BF16),
            pltpu.VMEM((slabs, slots, nb), F32),
            pltpu.VMEM((slabs, slots, nb), F32),
            pltpu.VMEM((slabs, slots, nb, nb), BF16),
            pltpu.SemaphoreType.DMA((5,)),
        ],
        input_output_aliases={8: 0, 9: 1},
        compiler_params=params(),
        name="section_vectors",
    )(where, rhs, previous, pin(below), pin(above), lower_gain, upper_gain, inverse_blocks, pin(keep), pin(send))

    recv = lax.ppermute(send, "stream", [(i, i ^ 1) for i in range(sections)])
    pair_keep, pair_send = pl.pallas_call(
        functools.partial(pair_kernel, slots, nv),
        out_shape=(one_shape, one_shape),
        in_specs=[SMEM, VMEM, VMEM],
        out_specs=(VMEM, VMEM),
        scratch_shapes=[index_scratch],
        compiler_params=params(),
        name="compose_chip",
    )(where, pin(keep), pin(recv))

    pair_recv = lax.ppermute(pair_send, "stream", [(i, i ^ 2) for i in range(sections)])
    group, state = pl.pallas_call(
        functools.partial(group_kernel, slots, nv),
        out_shape=(one_shape, vec_shape),
        in_specs=[SMEM, VMEM, VMEM],
        out_specs=(VMEM, VMEM),
        scratch_shapes=[index_scratch],
        compiler_params=params(),
        name="compose_group",
    )(where, pin(pair_keep), pin(pair_recv))

    hop = pl.pallas_call(
        functools.partial(hop_kernel, slots, nv),
        out_shape=(vec_shape, vec_shape),
        in_specs=[VMEM, VMEM, VMEM],
        out_specs=(VMEM, VMEM),
        scratch_shapes=[index_scratch],
        compiler_params=params(),
        name="hop",
    )
    inflow = jnp.zeros((slots, nv, nb), BF16)
    for g in range(1, groups):
        arrived = lax.ppermute(state, "stream", [(4 * g - 4 + r, 4 * g + r) for r in range(4)])
        state, inflow = hop(pin(arrived), pin(group), pin(inflow))

    shares = pl.pallas_call(
        functools.partial(share_kernel, slots, nv),
        out_shape=in_vmem((3, slots, nv, nb)),
        in_specs=[SMEM, VMEM, VMEM, VMEM, VMEM],
        out_specs=VMEM,
        scratch_shapes=[index_scratch],
        compiler_params=params(),
        name="share",
    )(where, pin(inflow), pin(pair_keep), pin(pair_recv), pin(group))
    shared = lax.all_gather(
        shares, "stream", axis_index_groups=[[4 * g + r for r in range(4)] for g in range(groups)]
    )
    return pl.pallas_call(
        functools.partial(finish_kernel, slots, nv),
        out_shape=jax.ShapeDtypeStruct(rhs.shape, BF16),
        in_specs=[SMEM, SMEM, VMEM, VMEM, VMEM],
        out_specs=VMEM,
        compiler_params=params(),
        name="finish",
    )(where, upstream_index, shared, pin(keep), pin(send))


def solution(mesh):
    in_specs = (
        P("stream", "span", None, None, None),
        P("stream", "span", None, None, None),
        P("stream", "span", None, None, None),
        P("stream", "span", None, None, None),
        P("stream", "span", None, None),
        P("stream", "span", None, None),
        P("stream"),
        P("stream", "span", None),
    )
    out_specs = P("stream", "span", None, None, None)
    return jax.shard_map(local, mesh=mesh, in_specs=in_specs, out_specs=out_specs, check_vma=False)
```

```python
import functools

import jax
import jax.numpy as jnp
from jax import lax
from jax.experimental import pallas as pl
from jax.experimental.pallas import tpu as pltpu
from jax.sharding import PartitionSpec as P

F32 = jnp.float32
BF16 = jnp.bfloat16
VMEM = pl.BlockSpec(memory_space=pltpu.VMEM)
SMEM = pl.BlockSpec(memory_space=pltpu.SMEM)
ANY = pl.BlockSpec(memory_space=pl.ANY)
PAD = 16


def pin(x):
    return pltpu.with_memory_space_constraint(x, pltpu.VMEM)


def in_hbm(x):
    return pltpu.with_memory_space_constraint(x, pltpu.HBM)


def in_vmem(shape, dtype=BF16):
    return pltpu.VMEM(shape, dtype)


def params(mib=16):
    return pltpu.CompilerParams(vmem_limit_bytes=mib * 1024 * 1024)


def cost(flops, size):
    return pl.CostEstimate(flops=flops, bytes_accessed=size, transcendentals=0)


def dot(a, b, dims=((1,), (0,))):
    return lax.dot_general(a, b, (dims, ((), ())), preferred_element_type=F32)


def place():
    position = lax.axis_index("stream")
    return lax.rem(position, 2), lax.rem(lax.div(position, 2), 2)


def maps_kernel(widths, rhs_hbm, prev_hbm, u_hbm, d_hbm, lower_hbm, upper_hbm, index_hbm, keep, send, d, partial,
                lower, upper, u, rhs, prev, lower_in, upper_in, index, u_sem, d_sem, sem):
    core, _ = place()
    slabs, slots, nv, nb = rhs.shape
    half = slabs // 2
    small = [
        pltpu.make_async_copy(index_hbm.at[0], index, sem.at[1]),
        pltpu.make_async_copy(lower_hbm.at[0], lower_in, sem.at[2]),
        pltpu.make_async_copy(upper_hbm.at[0], upper_in, sem.at[3]),
        pltpu.make_async_copy(prev_hbm.at[0], prev.at[pl.ds(1, slabs)], sem.at[4]),
        pltpu.make_async_copy(rhs_hbm.at[0], rhs, sem.at[0]),
    ]

    def block_copies(m):
        return (pltpu.make_async_copy(u_hbm.at[0, m], u.at[m], u_sem.at[m]),
                pltpu.make_async_copy(d_hbm.at[0, m], d.at[m], d_sem.at[m]))

    for copy in small:
        copy.start()
    for j in range(half):
        for first in ((1 - core) * half, core * half):
            for copy in block_copies(first + j):
                copy.start()
    prev[0] = jnp.zeros_like(prev[0])
    prev[slabs + 1] = jnp.zeros_like(prev[0])
    for copy in small:
        copy.wait()
    width = widths[0]
    rows = lax.broadcasted_iota(jnp.int32, (PAD, nb), 0)
    active = lax.broadcasted_iota(jnp.int32, (slots, nb), 0) < width

    def body(j, _):
        for out, first in ((send, (1 - core) * half), (keep, core * half)):
            m = first + j
            for copy in block_copies(m):
                copy.wait()
            tile = jnp.zeros((PAD, nb), F32)
            lo = jnp.where(active, lower_in[m], 0.0)
            up = jnp.where(active, upper_in[m], 0.0)
            lower[m], upper[m] = lo, up
            for k in range(slots):
                side = lo[k : k + 1, :] * prev[m, k].astype(F32) + up[k : k + 1, :] * prev[m + 2, k].astype(F32)
                part = jnp.where(k < width, rhs[m, k].astype(F32) - side, 0.0)
                partial[m, k] = part
                c = dot(part.astype(BF16), d[m, k], ((1,), (1,)))
                b = jnp.where(k < width, -dot(u[m, k], d[m, k], ((0,), (1,))), 0.0)
                out[j, pl.ds(k * (nv + nb), nv), :] = c.astype(BF16)
                out[j, pl.ds(k * (nv + nb) + nv, nb), :] = b.astype(BF16)
                tile = tile + jnp.where(rows == k, index[m, k].astype(F32), 0.0)
            out[j, pl.ds(slots * (nv + nb), PAD), :] = tile.astype(BF16)
        return 0

    lax.fori_loop(0, half, body, 0)


def edges_kernel(below, above, d, partial, lower, upper, keep_in, send_in, keep, send):
    core, _ = place()
    slabs, slots, nv, nb = partial.shape
    step = nv + nb

    def edge(out, j, m, gain, halo):
        for k in range(slots):
            part = partial[m, k] - gain[m, pl.ds(k, 1), :] * halo[0, k].astype(F32)
            out[j, pl.ds(k * step, nv), :] = dot(part.astype(BF16), d[m, k], ((1,), (1,))).astype(BF16)

    for here, first, last in ((0, keep, send), (1, send, keep)):
        @pl.when(core == here)
        def _():
            edge(first, 0, 0, lower, below)
            edge(last, slabs // 2 - 1, slabs - 1, upper, above)


def slot_scalars(tile, scratch, slots):
    scratch[...] = tile.astype(jnp.int32)
    return [scratch[k, 0] for k in range(slots)]


def compose(lo, hi, out, scratch, slots, nv, nb):
    step = nv + nb
    tile_lo = lo[pl.ds(slots * step, PAD), :].astype(F32)
    tile_hi = hi[pl.ds(slots * step, PAD), :].astype(F32)
    picks = slot_scalars(tile_hi, scratch, slots)
    tile = jnp.zeros_like(tile_hi)
    for n in range(slots):
        tile = tile + jnp.where(tile_hi == n, tile_lo[n : n + 1, :], 0.0)
    out[pl.ds(slots * step, PAD), :] = tile.astype(BF16)
    for k in range(slots):
        x = lo[pl.ds(pl.multiple_of(picks[k] * step, 16), step), :]
        y = dot(x, hi[pl.ds(k * step + nv, nb), :])
        c = hi[pl.ds(k * step, nv), :].astype(F32)
        out[pl.ds(k * step, nv), :] = (y[:nv] + c).astype(BF16)
        out[pl.ds(k * step + nv, nb), :] = y[nv:].astype(BF16)


def pair_kernel(slots, nv, keep, recv, out_keep, out_send, scratch):
    core, chip = place()
    nb = keep.shape[-1]
    for here, lo, hi in ((0, keep, recv), (1, recv, keep)):
        @pl.when(core == here)
        def _():
            compose(lo.at[1 - chip], hi.at[1 - chip], out_send, scratch, slots, nv, nb)
            compose(lo.at[chip], hi.at[chip], out_keep, scratch, slots, nv, nb)


def group_kernel(slots, nv, keep, recv, out, start, scratch):
    _, chip = place()
    nb = out.shape[-1]
    for here, lo, hi in ((0, keep, recv), (1, recv, keep)):
        @pl.when(chip == here)
        def _():
            compose(lo, hi, out, scratch, slots, nv, nb)
    for k in range(slots):
        start[k] = out[pl.ds(k * (nv + nb), nv), :]


def apply_map(x, m, out, scratch, slots, nv, nb):
    step = nv + nb
    picks = slot_scalars(m[pl.ds(slots * step, PAD), :].astype(F32), scratch, slots)
    for k in range(slots):
        y = dot(x[picks[k]], m[pl.ds(k * step + nv, nb), :])
        out[k] = (y + m[pl.ds(k * step, nv), :].astype(F32)).astype(BF16)


def hop_kernel(slots, nv, recv, group, inflow, out, inflow_out, scratch):
    apply_map(recv, group, out, scratch, slots, nv, group.shape[-1])
    inflow_out[...] = inflow[...] + recv[...]


def share_kernel(slots, nv, arrived, inflow, keep, recv, group, out, total, scratch):
    _, chip = place()
    nb = group.shape[-1]
    x = inflow[...] + arrived[...]
    total[...] = x
    out[0] = x
    for here, lo in ((0, keep), (1, recv)):
        @pl.when(chip == here)
        def _():
            apply_map(total, lo, out.at[1], scratch, slots, nv, nb)
    apply_map(total, group, out.at[2], scratch, slots, nv, nb)


def finish_kernel(slots, nv, shared, keep, send, out, result, scratch, sem):
    core, chip = place()
    slabs = out.shape[1]
    half = slabs // 2
    nb = out.shape[-1]
    owners = [2 * (m % 2) + m // 2 for m in range(slabs)]

    @pl.when(core == 1)
    def _():
        copies = [pltpu.make_async_copy(shared.at[owners[m], 1 + chip], out.at[0, m], sem.at[m]) for m in range(slabs)]
        for copy in copies:
            copy.start()
        for copy in copies:
            copy.wait()

    @pl.when(core == 0)
    def _():
        copies = []
        for m in range(slabs):
            maps = keep if m < half else send
            apply_map(shared.at[owners[m], chip], maps.at[m % half], result.at[m], scratch, slots, nv, nb)
            copies.append(pltpu.make_async_copy(result.at[m], out.at[0, m], sem.at[m]))
            copies[-1].start()
        for copy in copies:
            copy.wait()


def local(rhs, previous, inverse_blocks, upstream_blocks, lower_gain, upper_gain, widths, upstream_index):
    _, slabs, slots, nv, nb = rhs.shape
    half = slabs // 2
    sections, peers = lax.axis_size("stream"), lax.axis_size("span")
    groups = sections // 4
    rows = slots * (nv + nb) + PAD

    up = [(i, i + 1) for i in range(peers - 1)]
    down = [(j, i) for i, j in up]
    below = lax.ppermute(previous[0, slabs - 1 :], "span", up)
    above = lax.ppermute(previous[0, :1], "span", down)

    half_shape = in_vmem((half, rows, nb))
    one_shape = in_vmem((rows, nb))
    vec_shape = in_vmem((slots, nv, nb))
    index_scratch = pltpu.VMEM((PAD, nb), jnp.int32)
    block_shape, gain_shape = (slabs, slots, nb, nb), (slabs, slots, nb)

    keep, send, d, partial, lower, upper = pl.pallas_call(
        maps_kernel,
        out_shape=(half_shape, half_shape, in_vmem(block_shape), in_vmem((slabs, slots, nv, nb), F32),
                   in_vmem(gain_shape, F32), in_vmem(gain_shape, F32)),
        in_specs=[SMEM] + [ANY] * 7,
        out_specs=(VMEM,) * 6,
        scratch_shapes=[
            pltpu.VMEM(block_shape, BF16),
            pltpu.VMEM((slabs, slots, nv, nb), BF16),
            pltpu.VMEM((slabs + 2, slots, nv, nb), BF16),
            pltpu.VMEM(gain_shape, F32),
            pltpu.VMEM(gain_shape, F32),
            pltpu.SMEM((slabs, slots), jnp.int32),
            pltpu.SemaphoreType.DMA((slabs,)),
            pltpu.SemaphoreType.DMA((slabs,)),
            pltpu.SemaphoreType.DMA((5,)),
        ],
        compiler_params=params(),
        cost_estimate=cost(2 * slabs * slots * nb**3, 4 * slabs * slots * nb * nb),
        name="section_maps",
    )(widths, *(in_hbm(x) for x in (rhs, previous, upstream_blocks, inverse_blocks, lower_gain, upper_gain, upstream_index)))
    keep, send = pl.pallas_call(
        edges_kernel,
        out_shape=(half_shape, half_shape),
        in_specs=[VMEM] * 8,
        out_specs=(VMEM, VMEM),
        input_output_aliases={6: 0, 7: 1},
        compiler_params=params(),
        name="section_edges",
    )(*(pin(x) for x in (below, above, d, partial, lower, upper, keep, send)))

    recv = lax.ppermute(send, "stream", [(i, i ^ 1) for i in range(sections)])
    pair_keep, pair_send = pl.pallas_call(
        functools.partial(pair_kernel, slots, nv),
        out_shape=(one_shape, one_shape),
        in_specs=[VMEM, VMEM],
        out_specs=(VMEM, VMEM),
        scratch_shapes=[index_scratch],
        compiler_params=params(),
        name="compose_chip",
    )(pin(keep), pin(recv))

    pair_recv = lax.ppermute(pair_send, "stream", [(i, i ^ 2) for i in range(sections)])
    group, state = pl.pallas_call(
        functools.partial(group_kernel, slots, nv),
        out_shape=(one_shape, vec_shape),
        in_specs=[VMEM, VMEM],
        out_specs=(VMEM, VMEM),
        scratch_shapes=[index_scratch],
        compiler_params=params(),
        name="compose_group",
    )(pin(pair_keep), pin(pair_recv))

    hop = pl.pallas_call(
        functools.partial(hop_kernel, slots, nv),
        out_shape=(vec_shape, vec_shape),
        in_specs=[VMEM, VMEM, VMEM],
        out_specs=(VMEM, VMEM),
        scratch_shapes=[index_scratch],
        compiler_params=params(),
        name="hop",
    )
    inflow = jnp.zeros((slots, nv, nb), BF16)
    for g in range(1, groups):
        arrived = lax.ppermute(state, "stream", [(4 * g - 4 + r, 4 * g + r) for r in range(4)])
        if g < groups - 1:
            state, inflow = hop(pin(arrived), pin(group), pin(inflow))

    shares = pl.pallas_call(
        functools.partial(share_kernel, slots, nv),
        out_shape=in_vmem((3, slots, nv, nb)),
        in_specs=[VMEM] * 5,
        out_specs=VMEM,
        scratch_shapes=[pltpu.VMEM((slots, nv, nb), BF16), index_scratch],
        compiler_params=params(),
        name="share",
    )(pin(arrived), pin(inflow), pin(pair_keep), pin(pair_recv), pin(group))
    shared = lax.all_gather(
        shares, "stream", axis_index_groups=[[4 * g + r for r in range(4)] for g in range(groups)]
    )
    return pl.pallas_call(
        functools.partial(finish_kernel, slots, nv),
        out_shape=jax.ShapeDtypeStruct(rhs.shape, BF16),
        in_specs=[VMEM, VMEM, VMEM],
        out_specs=ANY,
        scratch_shapes=[
            pltpu.VMEM((slabs, slots, nv, nb), BF16),
            index_scratch,
            pltpu.SemaphoreType.DMA((slabs,)),
        ],
        compiler_params=params(),
        name="finish",
    )(pin(shared), pin(keep), pin(send))


def solution(mesh):
    in_specs = (
        P("stream", "span", None, None, None),
        P("stream", "span", None, None, None),
        P("stream", "span", None, None, None),
        P("stream", "span", None, None, None),
        P("stream", "span", None, None),
        P("stream", "span", None, None),
        P("stream"),
        P("stream", "span", None),
    )
    out_specs = P("stream", "span", None, None, None)
    return jax.shard_map(local, mesh=mesh, in_specs=in_specs, out_specs=out_specs, check_vma=False)
```

```python
import functools

import jax
import jax.numpy as jnp
from jax import lax
from jax.experimental import pallas as pl
from jax.experimental.pallas import tpu as pltpu
from jax.sharding import PartitionSpec as P

F32 = jnp.float32
BF16 = jnp.bfloat16
VMEM = pl.BlockSpec(memory_space=pltpu.VMEM)
ANY = pl.BlockSpec(memory_space=pl.ANY)
STEP = 4_600_000_000
PAD = 16
JOINED = (5, 6)


def pin(x):
    return pltpu.with_memory_space_constraint(x, pltpu.VMEM)


def in_hbm(x):
    return pltpu.with_memory_space_constraint(x, pltpu.HBM)


def in_vmem(shape, dtype=BF16):
    return pltpu.VMEM(shape, dtype)


def params(mib=16):
    return pltpu.CompilerParams(vmem_limit_bytes=mib * 1024 * 1024)


def cost(flops, size):
    return pl.CostEstimate(flops=flops, bytes_accessed=size, transcendentals=0)


def dot(a, b, dims=((1,), (0,))):
    return lax.dot_general(a, b, (dims, ((), ())), preferred_element_type=F32)


def place():
    position = lax.axis_index("stream")
    return lax.rem(position, 2), lax.rem(lax.div(position, 2), 2), lax.div(position, 4)


def front_half(chip, group):
    return jnp.logical_and(chip == 0, group == JOINED[1])


def back_half(chip, group):
    return jnp.logical_and(chip == 1, group == JOINED[0])


def maps_kernel(widths_hbm, rhs_hbm, prev_hbm, u_hbm, d_hbm, lower_hbm, upper_hbm, index_hbm, keep, send, d, partial,
                lower, upper, u, rhs, prev, lower_in, upper_in, index, widths, u_sem, d_sem, sem):
    core, _, _ = place()
    slabs, slots, nv, nb = rhs.shape
    half = slabs // 2
    small = [
        pltpu.make_async_copy(widths_hbm, widths, sem.at[5]),
        pltpu.make_async_copy(index_hbm.at[0], index, sem.at[1]),
        pltpu.make_async_copy(lower_hbm.at[0], lower_in, sem.at[2]),
        pltpu.make_async_copy(upper_hbm.at[0], upper_in, sem.at[3]),
        pltpu.make_async_copy(prev_hbm.at[0], prev.at[pl.ds(1, slabs)], sem.at[4]),
        pltpu.make_async_copy(rhs_hbm.at[0], rhs, sem.at[0]),
    ]

    def block_copies(m):
        return (pltpu.make_async_copy(u_hbm.at[0, m], u.at[m], u_sem.at[m]),
                pltpu.make_async_copy(d_hbm.at[0, m], d.at[m], d_sem.at[m]))

    for copy in small:
        copy.start()
    for j in range(half):
        for first in ((1 - core) * half, core * half):
            for copy in block_copies(first + j):
                copy.start()
    prev[0] = jnp.zeros_like(prev[0])
    prev[slabs + 1] = jnp.zeros_like(prev[0])
    for copy in small:
        copy.wait()
    width = widths[0]
    rows = lax.broadcasted_iota(jnp.int32, (PAD, nb), 0)
    active = lax.broadcasted_iota(jnp.int32, (slots, nb), 0) < width

    def body(j, _):
        for out, first in ((send, (1 - core) * half), (keep, core * half)):
            m = first + j
            for copy in block_copies(m):
                copy.wait()
            tile = jnp.zeros((PAD, nb), F32)
            lo = jnp.where(active, lower_in[m], 0.0)
            up = jnp.where(active, upper_in[m], 0.0)
            lower[m], upper[m] = lo, up
            for k in range(slots):
                side = lo[k : k + 1, :] * prev[m, k].astype(F32) + up[k : k + 1, :] * prev[m + 2, k].astype(F32)
                part = jnp.where(k < width, rhs[m, k].astype(F32) - side, 0.0)
                partial[m, k] = part
                c = dot(part.astype(BF16), d[m, k], ((1,), (1,)))
                b = jnp.where(k < width, -dot(u[m, k], d[m, k], ((0,), (1,))), 0.0)
                out[j, pl.ds(k * (nv + nb), nv), :] = c.astype(BF16)
                out[j, pl.ds(k * (nv + nb) + nv, nb), :] = b.astype(BF16)
                tile = tile + jnp.where(rows == k, index[m, k].astype(F32), 0.0)
            out[j, pl.ds(slots * (nv + nb), PAD), :] = tile.astype(BF16)
        return 0

    lax.fori_loop(0, half, body, 0)


def edges_kernel(below, above, d, partial, lower, upper, keep_in, send_in, keep, send):
    core, _, _ = place()
    slabs, slots, nv, nb = partial.shape
    step = nv + nb

    def edge(out, j, m, gain, halo):
        for k in range(slots):
            part = partial[m, k] - gain[m, pl.ds(k, 1), :] * halo[0, k].astype(F32)
            out[j, pl.ds(k * step, nv), :] = dot(part.astype(BF16), d[m, k], ((1,), (1,))).astype(BF16)

    for here, first, last in ((0, keep, send), (1, send, keep)):
        @pl.when(core == here)
        def _():
            edge(first, 0, 0, lower, below)
            edge(last, slabs // 2 - 1, slabs - 1, upper, above)


def slot_scalars(tile, scratch, slots):
    scratch[...] = tile.astype(jnp.int32)
    return [scratch[k, 0] for k in range(slots)]


def compose(lo, hi, out, scratch, slots, nv, nb):
    step = nv + nb
    tile_lo = lo[pl.ds(slots * step, PAD), :].astype(F32)
    tile_hi = hi[pl.ds(slots * step, PAD), :].astype(F32)
    picks = slot_scalars(tile_hi, scratch, slots)
    tile = jnp.zeros_like(tile_hi)
    for n in range(slots):
        tile = tile + jnp.where(tile_hi == n, tile_lo[n : n + 1, :], 0.0)
    out[pl.ds(slots * step, PAD), :] = tile.astype(BF16)
    for k in range(slots):
        x = lo[pl.ds(pl.multiple_of(picks[k] * step, 16), step), :]
        y = dot(x, hi[pl.ds(k * step + nv, nb), :])
        c = hi[pl.ds(k * step, nv), :].astype(F32)
        out[pl.ds(k * step, nv), :] = (y[:nv] + c).astype(BF16)
        out[pl.ds(k * step + nv, nb), :] = y[nv:].astype(BF16)


def pair_kernel(slots, nv, keep, recv, out_keep, out_send, start, scratch):
    core, chip, _ = place()
    nb = keep.shape[-1]
    for here, lo, hi in ((0, keep, recv), (1, recv, keep)):
        @pl.when(core == here)
        def _():
            compose(lo.at[1 - chip], hi.at[1 - chip], out_send, scratch, slots, nv, nb)
            compose(lo.at[chip], hi.at[chip], out_keep, scratch, slots, nv, nb)
    for k in range(slots):
        start[chip, k] = out_keep[pl.ds(k * (nv + nb), nv), :]
        start[1 - chip, k] = out_send[pl.ds(k * (nv + nb), nv), :]


def apply_map(x, m, out, scratch, slots, nv, nb):
    step = nv + nb
    picks = slot_scalars(m[pl.ds(slots * step, PAD), :].astype(F32), scratch, slots)
    for k in range(slots):
        y = dot(x[picks[k]], m[pl.ds(k * step + nv, nb), :])
        out[k] = (y + m[pl.ds(k * step, nv), :].astype(F32)).astype(BF16)


def first_kernel(slots, nv, arrived, keep, send, out_front, out_back, scratch):
    nb = keep.shape[-1]
    apply_map(arrived.at[0], send, out_front, scratch, slots, nv, nb)
    apply_map(arrived.at[1], keep, out_back, scratch, slots, nv, nb)


def second_kernel(slots, nv, front, back, keep, recv, state, inflow, middle, scratch):
    _, chip, _ = place()
    nb = keep.shape[-1]
    inflow[...] = front[...] + back[...]
    for here, lo, hi in ((0, keep, recv), (1, recv, keep)):
        @pl.when(chip == here)
        def _():
            apply_map(inflow, lo, middle, scratch, slots, nv, nb)
            apply_map(middle, hi, state, scratch, slots, nv, nb)


def group_kernel(slots, nv, keep, recv, out, scratch):
    _, chip, _ = place()
    nb = out.shape[-1]
    for here, lo, hi in ((0, keep, recv), (1, recv, keep)):
        @pl.when(chip == here)
        def _():
            compose(lo, hi, out, scratch, slots, nv, nb)


def join_kernel(slots, nv, group, recv, out, scratch):
    _, chip, number = place()
    nb = out.shape[-1]
    front, back = front_half(chip, number), back_half(chip, number)

    @pl.when(front)
    def _():
        compose(recv, group, out, scratch, slots, nv, nb)

    @pl.when(back)
    def _():
        compose(group, recv, out, scratch, slots, nv, nb)

    @pl.when(jnp.logical_not(jnp.logical_or(front, back)))
    def _():
        out[...] = group[...]


def hop_kernel(slots, nv, recv, chain, inflow, out, inflow_out, scratch):
    apply_map(recv, chain, out, scratch, slots, nv, chain.shape[-1])
    inflow_out[...] = inflow[...] + recv[...]


def fill_kernel(slots, nv, inflow, chain, group, out, scratch):
    _, chip, _ = place()
    for here, maps in ((0, chain), (1, group)):
        @pl.when(chip == here)
        def _():
            apply_map(inflow, maps, out, scratch, slots, nv, group.shape[-1])


def share_kernel(slots, nv, arrived, filled, inflow, joined, keep, recv, out, total, middle, scratch):
    _, chip, number = place()
    nb = keep.shape[-1]
    total[...] = inflow[...] + arrived[...] + filled[...]

    @pl.when(front_half(chip, number))
    def _():
        apply_map(total, joined, middle, scratch, slots, nv, nb)
        total[...] = middle[...]

    out[0] = total[...]
    for here, lo, hi in ((0, keep, recv), (1, recv, keep)):
        @pl.when(chip == here)
        def _():
            apply_map(total, lo, middle, scratch, slots, nv, nb)
            out[1] = middle[...]
            apply_map(middle, hi, out.at[2], scratch, slots, nv, nb)


def finish_kernel(slots, nv, shared, keep, send, out, result, scratch, sem):
    core, chip, _ = place()
    slabs = out.shape[1]
    half = slabs // 2
    nb = out.shape[-1]
    owners = [2 * (m % 2) + m // 2 for m in range(slabs)]

    @pl.when(core == 1)
    def _():
        copies = [pltpu.make_async_copy(shared.at[owners[m], 1 + chip], out.at[0, m], sem.at[m]) for m in range(slabs)]
        for copy in copies:
            copy.start()
        for copy in copies:
            copy.wait()

    @pl.when(core == 0)
    def _():
        copies = []
        for m in range(slabs):
            maps = keep if m < half else send
            apply_map(shared.at[owners[m], chip], maps.at[m % half], result.at[m], scratch, slots, nv, nb)
            copies.append(pltpu.make_async_copy(result.at[m], out.at[0, m], sem.at[m]))
            copies[-1].start()
        for copy in copies:
            copy.wait()


def local(rhs, previous, inverse_blocks, upstream_blocks, lower_gain, upper_gain, widths, upstream_index):
    _, slabs, slots, nv, nb = rhs.shape
    half = slabs // 2
    sections, peers = lax.axis_size("stream"), lax.axis_size("span")
    groups = sections // 4
    assert groups == JOINED[1] + 2
    rows = slots * (nv + nb) + PAD

    up = [(i, i + 1) for i in range(peers - 1)]
    down = [(j, i) for i, j in up]
    below = lax.ppermute(previous[0, slabs - 1 :], "span", up)
    above = lax.ppermute(previous[0, :1], "span", down)

    half_shape = in_vmem((half, rows, nb))
    one_shape = in_vmem((rows, nb))
    vec_shape = in_vmem((slots, nv, nb))
    index_scratch = pltpu.VMEM((PAD, nb), jnp.int32)
    block_shape, gain_shape = (slabs, slots, nb, nb), (slabs, slots, nb)

    keep, send, d, partial, lower, upper = pl.pallas_call(
        maps_kernel,
        out_shape=(half_shape, half_shape, in_vmem(block_shape), in_vmem((slabs, slots, nv, nb), F32),
                   in_vmem(gain_shape, F32), in_vmem(gain_shape, F32)),
        in_specs=[ANY] * 8,
        out_specs=(VMEM,) * 6,
        scratch_shapes=[
            pltpu.VMEM(block_shape, BF16),
            pltpu.VMEM((slabs, slots, nv, nb), BF16),
            pltpu.VMEM((slabs + 2, slots, nv, nb), BF16),
            pltpu.VMEM(gain_shape, F32),
            pltpu.VMEM(gain_shape, F32),
            pltpu.SMEM((slabs, slots), jnp.int32),
            pltpu.SMEM((1,), jnp.int32),
            pltpu.SemaphoreType.DMA((slabs,)),
            pltpu.SemaphoreType.DMA((slabs,)),
            pltpu.SemaphoreType.DMA((6,)),
        ],
        compiler_params=params(),
        cost_estimate=cost(2 * slabs * slots * nb**3, 4 * slabs * slots * nb * nb),
        name="section_maps",
    )(widths, *(in_hbm(x) for x in (rhs, previous, upstream_blocks, inverse_blocks, lower_gain, upper_gain, upstream_index)))
    keep, send = pl.pallas_call(
        edges_kernel,
        out_shape=(half_shape, half_shape),
        in_specs=[VMEM] * 8,
        out_specs=(VMEM, VMEM),
        input_output_aliases={6: 0, 7: 1},
        compiler_params=params(),
        name="section_edges",
    )(*(pin(x) for x in (below, above, d, partial, lower, upper, keep, send)))

    def call(kernel, outs, name, *args, scratch=(), flops=0):
        return pl.pallas_call(
            functools.partial(kernel, slots, nv),
            out_shape=outs,
            in_specs=[VMEM] * len(args),
            out_specs=(VMEM,) * len(outs) if isinstance(outs, tuple) else VMEM,
            scratch_shapes=[*scratch, index_scratch],
            compiler_params=params(),
            cost_estimate=cost(flops, 0) if flops else None,
            name=name,
        )(*(pin(x) for x in args))

    def stream(x, *hops):
        pairs = []
        for chip, source, target in hops:
            pairs += [(4 * source + 2 * chip + core, 4 * target + 2 * chip + core) for core in range(2)]
        return lax.ppermute(x, "stream", pairs)

    recv = lax.ppermute(send, "stream", [(i, i ^ 1) for i in range(sections)])
    pair_keep, pair_send, pair_start = call(
        pair_kernel, (one_shape, one_shape, in_vmem((2, slots, nv, nb))), "compose_chip", keep, recv)

    arrived = lax.ppermute(pair_start, "stream", [(0, 2), (1, 3)])
    recv_second = lax.ppermute(pair_send, "stream", [(i, i ^ 2) for i in range(4, 8)])
    recv_later = lax.ppermute(pair_send, "stream", [(i, i ^ 2) for i in range(8, sections)])
    front, back = call(first_kernel, (vec_shape, vec_shape), "first_group", arrived, pair_keep, pair_send, flops=STEP)
    back = lax.ppermute(back, "stream", [(2, 6), (3, 7)])
    front = lax.ppermute(front, "stream", [(2, 4), (3, 5)])
    state, inflow = call(
        second_kernel, (vec_shape, vec_shape), "second_group", front, back, pair_keep, recv_second, scratch=(vec_shape,), flops=STEP)
    arrived = stream(state, (0, 1, 2), (1, 1, 2))
    group = call(group_kernel, one_shape, "compose_group", pair_keep, recv_later, flops=STEP)

    a, b = JOINED
    join_recv = stream(group, (0, a, b), (1, b, a))
    for g in range(2, a):
        state, inflow = call(hop_kernel, (vec_shape, vec_shape), "hop", arrived, group, inflow, flops=STEP)
        arrived = stream(state, (0, g, g + 1 if g + 1 < a else b), (1, g, g + 1))
        if g == 2:
            pair_send, arrived = lax.optimization_barrier((pair_send, arrived))
            recv_first = lax.ppermute(pair_send, "stream", [(i, i ^ 2) for i in range(4)])
    chain = call(join_kernel, one_shape, "compose_join", group, join_recv)
    state, inflow = call(hop_kernel, (vec_shape, vec_shape), "hop", arrived, chain, inflow, flops=STEP)
    arrived = stream(state, (0, b, b + 1), (1, a, b + 1))
    passed = call(fill_kernel, vec_shape, "fill", inflow, chain, group)
    filled = stream(passed, (0, a - 1, a), (1, a, b))

    shares = call(
        share_kernel, in_vmem((3, slots, nv, nb)), "share",
        arrived, filled, inflow, join_recv, pair_keep, recv_first + recv_second + recv_later,
        scratch=(vec_shape, vec_shape))
    shared = lax.all_gather(
        shares, "stream", axis_index_groups=[[4 * g + r for r in range(4)] for g in range(groups)]
    )
    return pl.pallas_call(
        functools.partial(finish_kernel, slots, nv),
        out_shape=jax.ShapeDtypeStruct(rhs.shape, BF16),
        in_specs=[VMEM, VMEM, VMEM],
        out_specs=ANY,
        scratch_shapes=[
            pltpu.VMEM((slabs, slots, nv, nb), BF16),
            index_scratch,
            pltpu.SemaphoreType.DMA((slabs,)),
        ],
        compiler_params=params(),
        name="finish",
    )(pin(shared), pin(keep), pin(send))


def solution(mesh):
    in_specs = (
        P("stream", "span", None, None, None),
        P("stream", "span", None, None, None),
        P("stream", "span", None, None, None),
        P("stream", "span", None, None, None),
        P("stream", "span", None, None),
        P("stream", "span", None, None),
        P("stream"),
        P("stream", "span", None),
    )
    out_specs = P("stream", "span", None, None, None)
    return jax.shard_map(local, mesh=mesh, in_specs=in_specs, out_specs=out_specs, check_vma=False)
```

```python
import functools

import jax
import jax.numpy as jnp
from jax import lax
from jax.experimental import pallas as pl
from jax.experimental.pallas import tpu as pltpu
from jax.sharding import PartitionSpec as P

F32 = jnp.float32
BF16 = jnp.bfloat16
VMEM = pl.BlockSpec(memory_space=pltpu.VMEM)
ANY = pl.BlockSpec(memory_space=pl.ANY)
STEP = 4_600_000_000
PAD = 16
JOINED = (4, 5)


def pin(x):
    return pltpu.with_memory_space_constraint(x, pltpu.VMEM)


def in_hbm(x):
    return pltpu.with_memory_space_constraint(x, pltpu.HBM)


def in_vmem(shape, dtype=BF16):
    return pltpu.VMEM(shape, dtype)


def params(mib=16):
    return pltpu.CompilerParams(vmem_limit_bytes=mib * 1024 * 1024)


def cost(flops, size):
    return pl.CostEstimate(flops=flops, bytes_accessed=size, transcendentals=0)


def dot(a, b, dims=((1,), (0,))):
    return lax.dot_general(a, b, (dims, ((), ())), preferred_element_type=F32)


def place():
    position = lax.axis_index("stream")
    return lax.rem(position, 2), lax.rem(lax.div(position, 2), 2), lax.div(position, 4)


def front_half(chip, group):
    return jnp.logical_and(chip == 0, group == JOINED[1])


def back_half(chip, group):
    return jnp.logical_and(chip == 1, group == JOINED[0])


def last_group(group):
    return group == lax.div(lax.axis_size("stream"), 4) - 1


def outer_kernel(prev, last, first, sem):
    slabs = prev.shape[1]
    copies = [pltpu.make_async_copy(prev.at[0, pl.ds(slabs - 1, 1)], last, sem.at[0]),
              pltpu.make_async_copy(prev.at[0, pl.ds(0, 1)], first, sem.at[1])]
    for copy in copies:
        copy.start()
    for copy in copies:
        copy.wait()


def maps_kernel(widths_hbm, rhs_hbm, prev_hbm, u_hbm, d_hbm, lower_hbm, upper_hbm, index_hbm, keep, send, d, partial,
                lower, upper, u, rhs, prev, lower_in, upper_in, index, widths, u_sem, d_sem, sem):
    core, _, _ = place()
    slabs, slots, nv, nb = rhs.shape
    half = slabs // 2
    small = [
        pltpu.make_async_copy(widths_hbm, widths, sem.at[5]),
        pltpu.make_async_copy(index_hbm.at[0], index, sem.at[1]),
        pltpu.make_async_copy(lower_hbm.at[0], lower_in, sem.at[2]),
        pltpu.make_async_copy(upper_hbm.at[0], upper_in, sem.at[3]),
        pltpu.make_async_copy(prev_hbm.at[0], prev.at[pl.ds(1, slabs)], sem.at[4]),
        pltpu.make_async_copy(rhs_hbm.at[0], rhs, sem.at[0]),
    ]

    def block_copies(m):
        return (pltpu.make_async_copy(u_hbm.at[0, m], u.at[m], u_sem.at[m]),
                pltpu.make_async_copy(d_hbm.at[0, m], d.at[m], d_sem.at[m]))

    for copy in small:
        copy.start()
    for j in range(half):
        for first in ((1 - core) * half, core * half):
            for copy in block_copies(first + j):
                copy.start()
    prev[0] = jnp.zeros_like(prev[0])
    prev[slabs + 1] = jnp.zeros_like(prev[0])
    for copy in small:
        copy.wait()
    width = widths[0]
    rows = lax.broadcasted_iota(jnp.int32, (PAD, nb), 0)
    active = lax.broadcasted_iota(jnp.int32, (slots, nb), 0) < width

    def body(j, _):
        for out, first in ((send, (1 - core) * half), (keep, core * half)):
            m = first + j
            for copy in block_copies(m):
                copy.wait()
            tile = jnp.zeros((PAD, nb), F32)
            lo = jnp.where(active, lower_in[m], 0.0)
            up = jnp.where(active, upper_in[m], 0.0)
            lower[m], upper[m] = lo, up
            for k in range(slots):
                side = lo[k : k + 1, :] * prev[m, k].astype(F32) + up[k : k + 1, :] * prev[m + 2, k].astype(F32)
                part = jnp.where(k < width, rhs[m, k].astype(F32) - side, 0.0)
                partial[m, k] = part
                c = dot(part.astype(BF16), d[m, k], ((1,), (1,)))
                b = jnp.where(k < width, -dot(u[m, k], d[m, k], ((0,), (1,))), 0.0)
                out[j, pl.ds(k * (nv + nb), nv), :] = c.astype(BF16)
                out[j, pl.ds(k * (nv + nb) + nv, nb), :] = b.astype(BF16)
                tile = tile + jnp.where(rows == k, index[m, k].astype(F32), 0.0)
            out[j, pl.ds(slots * (nv + nb), PAD), :] = tile.astype(BF16)
        return 0

    lax.fori_loop(0, half, body, 0)


def edges_kernel(below, above, d, partial, lower, upper, keep_in, send_in, keep, send):
    core, _, _ = place()
    slabs, slots, nv, nb = partial.shape
    step = nv + nb

    def edge(out, j, m, gain, halo):
        for k in range(slots):
            part = partial[m, k] - gain[m, pl.ds(k, 1), :] * halo[0, k].astype(F32)
            out[j, pl.ds(k * step, nv), :] = dot(part.astype(BF16), d[m, k], ((1,), (1,))).astype(BF16)

    for here, first, last in ((0, keep, send), (1, send, keep)):
        @pl.when(core == here)
        def _():
            edge(first, 0, 0, lower, below)
            edge(last, slabs // 2 - 1, slabs - 1, upper, above)


def slot_scalars(tile, scratch, slots):
    scratch[...] = tile.astype(jnp.int32)
    return [scratch[k, 0] for k in range(slots)]


def compose(lo, hi, out, scratch, slots, nv, nb):
    step = nv + nb
    tile_lo = lo[pl.ds(slots * step, PAD), :].astype(F32)
    tile_hi = hi[pl.ds(slots * step, PAD), :].astype(F32)
    picks = slot_scalars(tile_hi, scratch, slots)
    tile = jnp.zeros_like(tile_hi)
    for n in range(slots):
        tile = tile + jnp.where(tile_hi == n, tile_lo[n : n + 1, :], 0.0)
    out[pl.ds(slots * step, PAD), :] = tile.astype(BF16)
    for k in range(slots):
        x = lo[pl.ds(pl.multiple_of(picks[k] * step, 16), step), :]
        y = dot(x, hi[pl.ds(k * step + nv, nb), :])
        c = hi[pl.ds(k * step, nv), :].astype(F32)
        out[pl.ds(k * step, nv), :] = (y[:nv] + c).astype(BF16)
        out[pl.ds(k * step + nv, nb), :] = y[nv:].astype(BF16)


def pair_kernel(slots, nv, keep, recv, out_keep, out_send, start, scratch):
    core, chip, _ = place()
    nb = keep.shape[-1]
    for here, lo, hi in ((0, keep, recv), (1, recv, keep)):
        @pl.when(core == here)
        def _():
            compose(lo.at[1 - chip], hi.at[1 - chip], out_send, scratch, slots, nv, nb)
            compose(lo.at[chip], hi.at[chip], out_keep, scratch, slots, nv, nb)
    for k in range(slots):
        start[chip, k] = out_keep[pl.ds(k * (nv + nb), nv), :]
        start[1 - chip, k] = out_send[pl.ds(k * (nv + nb), nv), :]


def apply_map(x, m, out, scratch, slots, nv, nb):
    step = nv + nb
    picks = slot_scalars(m[pl.ds(slots * step, PAD), :].astype(F32), scratch, slots)
    for k in range(slots):
        y = dot(x[picks[k]], m[pl.ds(k * step + nv, nb), :])
        out[k] = (y + m[pl.ds(k * step, nv), :].astype(F32)).astype(BF16)


def rest_kernel(slots, nv, even, odd, out, scratch):
    core, _, _ = place()
    half, _, nb = out.shape

    @pl.when(core == 1)
    def _():
        for j in range(half):
            compose(even.at[j], odd.at[j], out.at[j], scratch, slots, nv, nb)


def first_kernel(slots, nv, arrived, keep, send, out_front, out_back, scratch):
    nb = keep.shape[-1]
    apply_map(arrived.at[0], send, out_front, scratch, slots, nv, nb)
    apply_map(arrived.at[1], keep, out_back, scratch, slots, nv, nb)


def second_kernel(slots, nv, front, back, keep, recv, state, inflow, middle, scratch):
    _, chip, _ = place()
    nb = keep.shape[-1]
    inflow[...] = front[...] + back[...]
    for here, lo, hi in ((0, keep, recv), (1, recv, keep)):
        @pl.when(chip == here)
        def _():
            apply_map(inflow, lo, middle, scratch, slots, nv, nb)
            apply_map(middle, hi, state, scratch, slots, nv, nb)


def group_kernel(slots, nv, keep, recv, out, scratch):
    _, chip, _ = place()
    nb = out.shape[-1]
    for here, lo, hi in ((0, keep, recv), (1, recv, keep)):
        @pl.when(chip == here)
        def _():
            compose(lo, hi, out, scratch, slots, nv, nb)


def join_kernel(slots, nv, group, recv, out, scratch):
    _, chip, number = place()
    nb = out.shape[-1]
    front, back = front_half(chip, number), back_half(chip, number)

    @pl.when(front)
    def _():
        compose(recv, group, out, scratch, slots, nv, nb)

    @pl.when(back)
    def _():
        compose(group, recv, out, scratch, slots, nv, nb)

    @pl.when(jnp.logical_not(jnp.logical_or(front, back)))
    def _():
        out[...] = group[...]


def hop_kernel(slots, nv, recv, chain, inflow, out, inflow_out, scratch):
    apply_map(recv, chain, out, scratch, slots, nv, chain.shape[-1])
    inflow_out[...] = inflow[...] + recv[...]


def fill_kernel(slots, nv, inflow, chain, group, out, scratch):
    _, chip, _ = place()
    for here, maps in ((0, chain), (1, group)):
        @pl.when(chip == here)
        def _():
            apply_map(inflow, maps, out, scratch, slots, nv, group.shape[-1])


def share_kernel(slots, nv, arrived, passed, filled, inflow, joined, before_last, keep, recv, out, total, middle, scratch):
    _, chip, number = place()
    nb = keep.shape[-1]
    total[...] = inflow[...] + arrived[...] + passed[...] + filled[...]

    for condition, maps in ((front_half(chip, number), joined), (last_group(number), before_last)):
        @pl.when(condition)
        def _():
            apply_map(total, maps, middle, scratch, slots, nv, nb)
            total[...] = middle[...]

    out[0] = total[...]
    for here, lo in ((0, keep), (1, recv)):
        @pl.when(chip == here)
        def _():
            apply_map(total, lo, out.at[1], scratch, slots, nv, nb)


def finish_kernel(slots, nv, shared, keep, send, rest, pair_keep, pair_send, out, result, scratch, sem):
    core, chip, _ = place()
    slabs, nb = out.shape[1], out.shape[-1]
    half = slabs // 2
    even = [(keep if m < half else send).at[m % half] for m in range(slabs)]
    odd = [rest.at[m] for m in range(half)]
    for condition, maps in (
        (core == 0, even),
        (jnp.logical_and(core == 1, chip == 0), [*odd, pair_keep, pair_send]),
        (jnp.logical_and(core == 1, chip == 1), [*odd, pair_send, pair_keep]),
    ):
        @pl.when(condition)
        def _():
            copies = []
            for m in range(slabs):
                x = shared.at[2 * (m % 2) + m // 2, chip]
                apply_map(x, maps[m], result.at[m], scratch, slots, nv, nb)
                copies.append(pltpu.make_async_copy(result.at[m], out.at[0, m], sem.at[m]))
                copies[-1].start()
            for copy in copies:
                copy.wait()


def local(rhs, previous, inverse_blocks, upstream_blocks, lower_gain, upper_gain, widths, upstream_index):
    _, slabs, slots, nv, nb = rhs.shape
    half = slabs // 2
    sections, peers = lax.axis_size("stream"), lax.axis_size("span")
    groups = sections // 4
    assert groups > JOINED[1] + 2
    rows = slots * (nv + nb) + PAD

    up = [(i, i + 1) for i in range(peers - 1)]
    down = [(j, i) for i, j in up]
    edge_shape = in_vmem((1, slots, nv, nb))
    last_slab, first_slab = pl.pallas_call(
        outer_kernel,
        out_shape=(edge_shape, edge_shape),
        in_specs=[ANY],
        out_specs=(VMEM, VMEM),
        scratch_shapes=[pltpu.SemaphoreType.DMA((2,))],
        compiler_params=params(),
        name="outer_slabs",
    )(in_hbm(previous))
    below = lax.ppermute(last_slab, "span", up)
    above = lax.ppermute(first_slab, "span", down)

    half_shape = in_vmem((half, rows, nb))
    one_shape = in_vmem((rows, nb))
    vec_shape = in_vmem((slots, nv, nb))
    index_scratch = pltpu.VMEM((PAD, nb), jnp.int32)
    block_shape, gain_shape = (slabs, slots, nb, nb), (slabs, slots, nb)

    keep, send, d, partial, lower, upper = pl.pallas_call(
        maps_kernel,
        out_shape=(half_shape, half_shape, in_vmem(block_shape), in_vmem((slabs, slots, nv, nb), F32),
                   in_vmem(gain_shape, F32), in_vmem(gain_shape, F32)),
        in_specs=[ANY] * 8,
        out_specs=(VMEM,) * 6,
        scratch_shapes=[
            pltpu.VMEM(block_shape, BF16),
            pltpu.VMEM((slabs, slots, nv, nb), BF16),
            pltpu.VMEM((slabs + 2, slots, nv, nb), BF16),
            pltpu.VMEM(gain_shape, F32),
            pltpu.VMEM(gain_shape, F32),
            pltpu.SMEM((slabs, slots), jnp.int32),
            pltpu.SMEM((1,), jnp.int32),
            pltpu.SemaphoreType.DMA((slabs,)),
            pltpu.SemaphoreType.DMA((slabs,)),
            pltpu.SemaphoreType.DMA((6,)),
        ],
        compiler_params=params(),
        cost_estimate=cost(2 * slabs * slots * nb**3, 4 * slabs * slots * nb * nb),
        name="section_maps",
    )(widths, *(in_hbm(x) for x in (rhs, previous, upstream_blocks, inverse_blocks, lower_gain, upper_gain, upstream_index)))
    keep, send = pl.pallas_call(
        edges_kernel,
        out_shape=(half_shape, half_shape),
        in_specs=[VMEM] * 8,
        out_specs=(VMEM, VMEM),
        input_output_aliases={6: 0, 7: 1},
        compiler_params=params(),
        name="section_edges",
    )(*(pin(x) for x in (below, above, d, partial, lower, upper, keep, send)))

    def call(kernel, outs, name, *args, scratch=(), flops=0):
        return pl.pallas_call(
            functools.partial(kernel, slots, nv),
            out_shape=outs,
            in_specs=[VMEM] * len(args),
            out_specs=(VMEM,) * len(outs) if isinstance(outs, tuple) else VMEM,
            scratch_shapes=[*scratch, index_scratch],
            compiler_params=params(),
            cost_estimate=cost(flops, 0) if flops else None,
            name=name,
        )(*(pin(x) for x in args))

    def stream(x, *hops):
        pairs = []
        for chip, source, target in hops:
            pairs += [(4 * source + 2 * chip + core, 4 * target + 2 * chip + core) for core in range(2)]
        return lax.ppermute(x, "stream", pairs)

    recv = lax.ppermute(send, "stream", [(i, i ^ 1) for i in range(sections)])
    pair_keep, pair_send, pair_start = call(
        pair_kernel, (one_shape, one_shape, in_vmem((2, slots, nv, nb))), "compose_chip", keep, recv)

    arrived = lax.ppermute(pair_start, "stream", [(0, 2), (1, 3)])
    recv_second = lax.ppermute(pair_send, "stream", [(i, i ^ 2) for i in range(4, 8)])
    recv_later = lax.ppermute(pair_send, "stream", [(i, i ^ 2) for i in range(8, sections)])
    front, back = call(first_kernel, (vec_shape, vec_shape), "first_group", arrived, pair_keep, pair_send, flops=STEP)
    back = lax.ppermute(back, "stream", [(2, 6), (3, 7)])
    front = lax.ppermute(front, "stream", [(2, 4), (3, 5)])
    state, inflow = call(
        second_kernel, (vec_shape, vec_shape), "second_group", front, back, pair_keep, recv_second, scratch=(vec_shape,), flops=STEP)
    arrived = stream(state, (0, 1, 2), (1, 1, 2))
    group = call(group_kernel, one_shape, "compose_group", pair_keep, recv_later, flops=STEP)

    keep_again, state = lax.optimization_barrier((keep, state))
    even = lax.ppermute(keep_again, "stream", [(i, i + 1) for i in range(0, sections, 2)])
    rest = call(rest_kernel, half_shape, "compose_rest", even, send, flops=STEP)

    a, b = JOINED
    last = groups - 1
    join_recv = stream(group, (0, a, b), (1, b, a))
    last_recv = stream(group, (0, last - 1, last), (1, last - 1, last))
    chain = call(join_kernel, one_shape, "compose_join", group, join_recv)
    chain, rest = lax.optimization_barrier((chain, rest))
    steps = [(2, 2), *((g, g) for g in range(3, a)), (b, a), *((g, g) for g in range(b + 1, last - 1))]
    for step, (front, back) in enumerate(steps):
        maps = group if front < a else chain
        state, inflow = call(hop_kernel, (vec_shape, vec_shape), "hop", arrived, maps, inflow, flops=STEP)
        if step + 1 < len(steps):
            arrived = stream(state, (0, front, steps[step + 1][0]), (1, back, steps[step + 1][1]))
        else:
            arrived = stream(state, (0, front, last), (1, back, last))
            passed = stream(state, (0, front, last - 1), (1, back, last - 1))
        if step == 0:
            pair_send_later, arrived = lax.optimization_barrier((pair_send, arrived))
            recv_first = lax.ppermute(pair_send_later, "stream", [(i, i ^ 2) for i in range(4)])
    filled = stream(call(fill_kernel, vec_shape, "fill", inflow, chain, group), (0, a - 1, a), (1, a, b))

    shares = call(
        share_kernel, in_vmem((2, slots, nv, nb)), "share",
        arrived, passed, filled, inflow, join_recv, last_recv, pair_keep, recv_first + recv_second + recv_later,
        scratch=(vec_shape, vec_shape))
    shared = lax.all_gather(
        shares, "stream", axis_index_groups=[[4 * g + r for r in range(4)] for g in range(groups)]
    )
    return pl.pallas_call(
        functools.partial(finish_kernel, slots, nv),
        out_shape=jax.ShapeDtypeStruct(rhs.shape, BF16),
        in_specs=[VMEM] * 6,
        out_specs=ANY,
        scratch_shapes=[
            pltpu.VMEM((slabs, slots, nv, nb), BF16),
            index_scratch,
            pltpu.SemaphoreType.DMA((slabs,)),
        ],
        compiler_params=params(),
        name="finish",
    )(*(pin(x) for x in (shared, keep, send, rest, pair_keep, pair_send)))


def solution(mesh):
    in_specs = (
        P("stream", "span", None, None, None),
        P("stream", "span", None, None, None),
        P("stream", "span", None, None, None),
        P("stream", "span", None, None, None),
        P("stream", "span", None, None),
        P("stream", "span", None, None),
        P("stream"),
        P("stream", "span", None),
    )
    out_specs = P("stream", "span", None, None, None)
    return jax.shard_map(local, mesh=mesh, in_specs=in_specs, out_specs=out_specs, check_vma=False)
```

```python
import functools

import jax
import jax.numpy as jnp
from jax import lax
from jax.experimental import pallas as pl
from jax.experimental.pallas import tpu as pltpu
from jax.sharding import PartitionSpec as P

F32 = jnp.float32
BF16 = jnp.bfloat16
VMEM = pl.BlockSpec(memory_space=pltpu.VMEM)
ANY = pl.BlockSpec(memory_space=pl.ANY)
STEP = 2_300_000_000
PAD = 16
JOINED = (4, 5)


def pin(x):
    return pltpu.with_memory_space_constraint(x, pltpu.VMEM)


def in_hbm(x):
    return pltpu.with_memory_space_constraint(x, pltpu.HBM)


def in_vmem(shape, dtype=BF16):
    return pltpu.VMEM(shape, dtype)


def params(mib=16):
    return pltpu.CompilerParams(vmem_limit_bytes=mib * 1024 * 1024)


def cost(flops, size):
    return pl.CostEstimate(flops=flops, bytes_accessed=size, transcendentals=0)


def dot(a, b, dims=((1,), (0,))):
    return lax.dot_general(a, b, (dims, ((), ())), preferred_element_type=F32)


def place():
    position = lax.axis_index("stream")
    return lax.rem(position, 2), lax.rem(lax.div(position, 2), 2), lax.div(position, 4)


def front_half(chip, group):
    return jnp.logical_and(chip == 0, group == JOINED[1])


def back_half(chip, group):
    return jnp.logical_and(chip == 1, group == JOINED[0])


def last_group(group):
    return group == lax.div(lax.axis_size("stream"), 4) - 1


def outer_kernel(prev, last, first, sem):
    slabs = prev.shape[1]
    copies = [pltpu.make_async_copy(prev.at[0, pl.ds(slabs - 1, 1)], last, sem.at[0]),
              pltpu.make_async_copy(prev.at[0, pl.ds(0, 1)], first, sem.at[1])]
    for copy in copies:
        copy.start()
    for copy in copies:
        copy.wait()


def maps_kernel(widths_hbm, rhs_hbm, prev_hbm, u_hbm, d_hbm, lower_hbm, upper_hbm, index_hbm, keep, send, d, partial,
                lower, upper, u, rhs, prev, lower_in, upper_in, index, widths, u_sem, d_sem, sem):
    core, _, _ = place()
    slabs, slots, nv, nb = rhs.shape
    half = slabs // 2
    small = [
        pltpu.make_async_copy(widths_hbm, widths, sem.at[5]),
        pltpu.make_async_copy(index_hbm.at[0], index, sem.at[1]),
        pltpu.make_async_copy(lower_hbm.at[0], lower_in, sem.at[2]),
        pltpu.make_async_copy(upper_hbm.at[0], upper_in, sem.at[3]),
        pltpu.make_async_copy(prev_hbm.at[0], prev.at[pl.ds(1, slabs)], sem.at[4]),
        pltpu.make_async_copy(rhs_hbm.at[0], rhs, sem.at[0]),
    ]

    def block_copies(m):
        return (pltpu.make_async_copy(u_hbm.at[0, m], u.at[m], u_sem.at[m]),
                pltpu.make_async_copy(d_hbm.at[0, m], d.at[m], d_sem.at[m]))

    for copy in small:
        copy.start()
    for j in range(half):
        for first in ((1 - core) * half, core * half):
            for copy in block_copies(first + j):
                copy.start()
    prev[0] = jnp.zeros_like(prev[0])
    prev[slabs + 1] = jnp.zeros_like(prev[0])
    for copy in small:
        copy.wait()
    width = widths[0]
    rows = lax.broadcasted_iota(jnp.int32, (PAD, nb), 0)
    active = lax.broadcasted_iota(jnp.int32, (slots, nb), 0) < width

    def body(j, _):
        for out, first in ((send, (1 - core) * half), (keep, core * half)):
            m = first + j
            for copy in block_copies(m):
                copy.wait()
            tile = jnp.zeros((PAD, nb), F32)
            lo = jnp.where(active, lower_in[m], 0.0)
            up = jnp.where(active, upper_in[m], 0.0)
            lower[m], upper[m] = lo, up
            for k in range(slots):
                side = lo[k : k + 1, :] * prev[m, k].astype(F32) + up[k : k + 1, :] * prev[m + 2, k].astype(F32)
                part = jnp.where(k < width, rhs[m, k].astype(F32) - side, 0.0)
                partial[m, k] = part
                c = dot(part.astype(BF16), d[m, k], ((1,), (1,)))
                b = jnp.where(k < width, -dot(u[m, k], d[m, k], ((0,), (1,))), 0.0)
                out[j, pl.ds(k * (nv + nb), nv), :] = c.astype(BF16)
                out[j, pl.ds(k * (nv + nb) + nv, nb), :] = b.astype(BF16)
                tile = tile + jnp.where(rows == k, index[m, k].astype(F32), 0.0)
            out[j, pl.ds(slots * (nv + nb), PAD), :] = tile.astype(BF16)
        return 0

    lax.fori_loop(0, half, body, 0)


def edges_kernel(below, above, d, partial, lower, upper, keep_in, send_in, keep, send):
    core, _, _ = place()
    slabs, slots, nv, nb = partial.shape
    step = nv + nb

    def edge(out, j, m, gain, halo):
        for k in range(slots):
            part = partial[m, k] - gain[m, pl.ds(k, 1), :] * halo[0, k].astype(F32)
            out[j, pl.ds(k * step, nv), :] = dot(part.astype(BF16), d[m, k], ((1,), (1,))).astype(BF16)

    for here, first, last in ((0, keep, send), (1, send, keep)):
        @pl.when(core == here)
        def _():
            edge(first, 0, 0, lower, below)
            edge(last, slabs // 2 - 1, slabs - 1, upper, above)


def slot_scalars(tile, scratch, slots):
    scratch[...] = tile.astype(jnp.int32)
    return [scratch[k, 0] for k in range(slots)]


def compose(lo, hi, out, scratch, slots, nv, nb):
    step = nv + nb
    tile_lo = lo[pl.ds(slots * step, PAD), :].astype(F32)
    tile_hi = hi[pl.ds(slots * step, PAD), :].astype(F32)
    picks = slot_scalars(tile_hi, scratch, slots)
    tile = jnp.zeros_like(tile_hi)
    for n in range(slots):
        tile = tile + jnp.where(tile_hi == n, tile_lo[n : n + 1, :], 0.0)
    out[pl.ds(slots * step, PAD), :] = tile.astype(BF16)
    for k in range(slots):
        x = lo[pl.ds(pl.multiple_of(picks[k] * step, 16), step), :]
        y = dot(x, hi[pl.ds(k * step + nv, nb), :])
        c = hi[pl.ds(k * step, nv), :].astype(F32)
        out[pl.ds(k * step, nv), :] = (y[:nv] + c).astype(BF16)
        out[pl.ds(k * step + nv, nb), :] = y[nv:].astype(BF16)


def pair_kernel(slots, nv, keep, recv, out_keep, out_send, start, scratch):
    core, chip, _ = place()
    nb = keep.shape[-1]
    for here, lo, hi in ((0, keep, recv), (1, recv, keep)):
        @pl.when(core == here)
        def _():
            compose(lo.at[1 - chip], hi.at[1 - chip], out_send, scratch, slots, nv, nb)
            compose(lo.at[chip], hi.at[chip], out_keep, scratch, slots, nv, nb)
    for k in range(slots):
        start[chip, k] = out_keep[pl.ds(k * (nv + nb), nv), :]
        start[1 - chip, k] = out_send[pl.ds(k * (nv + nb), nv), :]


def apply_map(x, m, out, scratch, slots, nv, nb):
    step = nv + nb
    picks = slot_scalars(m[pl.ds(slots * step, PAD), :].astype(F32), scratch, slots)
    for k in range(slots):
        y = dot(x[picks[k]], m[pl.ds(k * step + nv, nb), :])
        out[k] = (y + m[pl.ds(k * step, nv), :].astype(F32)).astype(BF16)


def rest_kernel(slots, nv, even, odd, out, scratch):
    core, _, _ = place()
    half, _, nb = out.shape

    @pl.when(core == 1)
    def _():
        for j in range(half):
            compose(even.at[j], odd.at[j], out.at[j], scratch, slots, nv, nb)


def first_kernel(slots, nv, arrived, keep, send, out_front, out_back, scratch):
    nb = keep.shape[-1]
    apply_map(arrived.at[0], send, out_front, scratch, slots, nv, nb)
    apply_map(arrived.at[1], keep, out_back, scratch, slots, nv, nb)


def second_kernel(slots, nv, front, back, keep, recv, state, inflow, middle, scratch):
    _, chip, _ = place()
    nb = keep.shape[-1]
    inflow[...] = front[...] + back[...]
    for here, lo, hi in ((0, keep, recv), (1, recv, keep)):
        @pl.when(chip == here)
        def _():
            apply_map(inflow, lo, middle, scratch, slots, nv, nb)
            apply_map(middle, hi, state, scratch, slots, nv, nb)


def group_kernel(slots, nv, keep, recv, out, scratch):
    _, chip, _ = place()
    nb = out.shape[-1]
    for here, lo, hi in ((0, keep, recv), (1, recv, keep)):
        @pl.when(chip == here)
        def _():
            compose(lo, hi, out, scratch, slots, nv, nb)


def join_kernel(slots, nv, group, recv, out, scratch):
    _, chip, number = place()
    nb = out.shape[-1]
    front, back = front_half(chip, number), back_half(chip, number)

    @pl.when(front)
    def _():
        compose(recv, group, out, scratch, slots, nv, nb)

    @pl.when(back)
    def _():
        compose(group, recv, out, scratch, slots, nv, nb)

    @pl.when(jnp.logical_not(jnp.logical_or(front, back)))
    def _():
        out[...] = group[...]


def hop_kernel(slots, nv, recv, chain, inflow, out, inflow_out, scratch):
    apply_map(recv, chain, out, scratch, slots, nv, chain.shape[-1])
    inflow_out[...] = inflow[...] + recv[...]


def fill_kernel(slots, nv, inflow, chain, group, out, scratch):
    _, chip, _ = place()
    for here, maps in ((0, chain), (1, group)):
        @pl.when(chip == here)
        def _():
            apply_map(inflow, maps, out, scratch, slots, nv, group.shape[-1])


def share_kernel(slots, nv, arrived, passed, filled, inflow, joined, before_last, keep, recv, out, total, middle, scratch):
    _, chip, number = place()
    nb = keep.shape[-1]
    total[...] = inflow[...] + arrived[...] + passed[...] + filled[...]

    for condition, maps in ((front_half(chip, number), joined), (last_group(number), before_last)):
        @pl.when(condition)
        def _():
            apply_map(total, maps, middle, scratch, slots, nv, nb)
            total[...] = middle[...]

    out[0] = total[...]
    for here, lo in ((0, keep), (1, recv)):
        @pl.when(chip == here)
        def _():
            apply_map(total, lo, out.at[1], scratch, slots, nv, nb)


def finish_kernel(slots, nv, shared, keep, send, rest, pair_keep, pair_send, out, result, scratch, sem):
    core, chip, _ = place()
    slabs, nb = out.shape[1], out.shape[-1]
    half = slabs // 2
    even = [(keep if m < half else send).at[m % half] for m in range(slabs)]
    odd = [rest.at[m] for m in range(half)]
    for condition, maps in (
        (core == 0, even),
        (jnp.logical_and(core == 1, chip == 0), [*odd, pair_keep, pair_send]),
        (jnp.logical_and(core == 1, chip == 1), [*odd, pair_send, pair_keep]),
    ):
        @pl.when(condition)
        def _():
            copies = []
            for m in range(slabs):
                x = shared.at[2 * (m % 2) + m // 2, chip]
                apply_map(x, maps[m], result.at[m], scratch, slots, nv, nb)
                copies.append(pltpu.make_async_copy(result.at[m], out.at[0, m], sem.at[m]))
                copies[-1].start()
            for copy in copies:
                copy.wait()


def local(rhs, previous, inverse_blocks, upstream_blocks, lower_gain, upper_gain, widths, upstream_index):
    _, slabs, slots, nv, nb = rhs.shape
    half = slabs // 2
    sections, peers = lax.axis_size("stream"), lax.axis_size("span")
    groups = sections // 4
    assert groups > JOINED[1] + 2
    rows = slots * (nv + nb) + PAD

    up = [(i, i + 1) for i in range(peers - 1)]
    down = [(j, i) for i, j in up]
    edge_shape = in_vmem((1, slots, nv, nb))
    last_slab, first_slab = pl.pallas_call(
        outer_kernel,
        out_shape=(edge_shape, edge_shape),
        in_specs=[ANY],
        out_specs=(VMEM, VMEM),
        scratch_shapes=[pltpu.SemaphoreType.DMA((2,))],
        compiler_params=params(),
        name="outer_slabs",
    )(in_hbm(previous))
    below = lax.ppermute(last_slab, "span", up)
    above = lax.ppermute(first_slab, "span", down)

    half_shape = in_vmem((half, rows, nb))
    one_shape = in_vmem((rows, nb))
    vec_shape = in_vmem((slots, nv, nb))
    index_scratch = pltpu.VMEM((PAD, nb), jnp.int32)
    block_shape, gain_shape = (slabs, slots, nb, nb), (slabs, slots, nb)

    keep, send, d, partial, lower, upper = pl.pallas_call(
        maps_kernel,
        out_shape=(half_shape, half_shape, in_vmem(block_shape), in_vmem((slabs, slots, nv, nb), F32),
                   in_vmem(gain_shape, F32), in_vmem(gain_shape, F32)),
        in_specs=[ANY] * 8,
        out_specs=(VMEM,) * 6,
        scratch_shapes=[
            pltpu.VMEM(block_shape, BF16),
            pltpu.VMEM((slabs, slots, nv, nb), BF16),
            pltpu.VMEM((slabs + 2, slots, nv, nb), BF16),
            pltpu.VMEM(gain_shape, F32),
            pltpu.VMEM(gain_shape, F32),
            pltpu.SMEM((slabs, slots), jnp.int32),
            pltpu.SMEM((1,), jnp.int32),
            pltpu.SemaphoreType.DMA((slabs,)),
            pltpu.SemaphoreType.DMA((slabs,)),
            pltpu.SemaphoreType.DMA((6,)),
        ],
        compiler_params=params(),
        cost_estimate=cost(2 * slabs * slots * nb**3, 4 * slabs * slots * nb * nb),
        name="section_maps",
    )(widths, *(in_hbm(x) for x in (rhs, previous, upstream_blocks, inverse_blocks, lower_gain, upper_gain, upstream_index)))
    keep, send = pl.pallas_call(
        edges_kernel,
        out_shape=(half_shape, half_shape),
        in_specs=[VMEM] * 8,
        out_specs=(VMEM, VMEM),
        input_output_aliases={6: 0, 7: 1},
        compiler_params=params(),
        name="section_edges",
    )(*(pin(x) for x in (below, above, d, partial, lower, upper, keep, send)))

    def call(kernel, outs, name, *args, scratch=(), flops=0):
        return pl.pallas_call(
            functools.partial(kernel, slots, nv),
            out_shape=outs,
            in_specs=[VMEM] * len(args),
            out_specs=(VMEM,) * len(outs) if isinstance(outs, tuple) else VMEM,
            scratch_shapes=[*scratch, index_scratch],
            compiler_params=params(),
            cost_estimate=cost(flops, 0) if flops else None,
            name=name,
        )(*(pin(x) for x in args))

    def stream(x, *hops):
        pairs = []
        for chip, source, target in hops:
            pairs += [(4 * source + 2 * chip + core, 4 * target + 2 * chip + core) for core in range(2)]
        return lax.ppermute(x, "stream", pairs)

    recv = lax.ppermute(send, "stream", [(i, i ^ 1) for i in range(sections)])
    pair_keep, pair_send, pair_start = call(
        pair_kernel, (one_shape, one_shape, in_vmem((2, slots, nv, nb))), "compose_chip", keep, recv)

    arrived = lax.ppermute(pair_start, "stream", [(0, 2), (1, 3)])
    recv_second = lax.ppermute(pair_send, "stream", [(i, i ^ 2) for i in range(4, 8)])
    recv_later = lax.ppermute(pair_send, "stream", [(i, i ^ 2) for i in range(8, sections)])
    front, back = call(first_kernel, (vec_shape, vec_shape), "first_group", arrived, pair_keep, pair_send, flops=STEP)
    back = lax.ppermute(back, "stream", [(2, 6), (3, 7)])
    front = lax.ppermute(front, "stream", [(2, 4), (3, 5)])
    state, inflow = call(
        second_kernel, (vec_shape, vec_shape), "second_group", front, back, pair_keep, recv_second, scratch=(vec_shape,), flops=STEP)
    arrived = stream(state, (0, 1, 2), (1, 1, 2))
    group = call(group_kernel, one_shape, "compose_group", pair_keep, recv_later, flops=STEP)

    keep_again, pair_send_again, state = lax.optimization_barrier((keep, pair_send, state))
    recv_first = lax.ppermute(pair_send_again, "stream", [(i, i ^ 2) for i in range(4)])
    even = lax.ppermute(keep_again, "stream", [(i, i + 1) for i in range(0, sections, 2)])
    rest = call(rest_kernel, half_shape, "compose_rest", even, send, flops=STEP)

    a, b = JOINED
    last = groups - 1
    join_recv = stream(group, (0, a, b), (1, b, a))
    last_recv = stream(group, (0, last - 1, last), (1, last - 1, last))
    chain = call(join_kernel, one_shape, "compose_join", group, join_recv)
    chain, rest = lax.optimization_barrier((chain, rest))
    steps = [(2, 2), *((g, g) for g in range(3, a)), (b, a), *((g, g) for g in range(b + 1, last - 1))]
    for step, (front, back) in enumerate(steps):
        maps = group if front < a else chain
        state, inflow = call(hop_kernel, (vec_shape, vec_shape), "hop", arrived, maps, inflow, flops=STEP)
        if step + 1 < len(steps):
            arrived = stream(state, (0, front, steps[step + 1][0]), (1, back, steps[step + 1][1]))
        else:
            arrived = stream(state, (0, front, last), (1, back, last))
            passed = stream(state, (0, front, last - 1), (1, back, last - 1))
    filled = stream(call(fill_kernel, vec_shape, "fill", inflow, chain, group), (0, a - 1, a), (1, a, b))

    shares = call(
        share_kernel, in_vmem((2, slots, nv, nb)), "share",
        arrived, passed, filled, inflow, join_recv, last_recv, pair_keep, recv_first + recv_second + recv_later,
        scratch=(vec_shape, vec_shape))
    shared = lax.all_gather(
        shares, "stream", axis_index_groups=[[4 * g + r for r in range(4)] for g in range(groups)]
    )
    return pl.pallas_call(
        functools.partial(finish_kernel, slots, nv),
        out_shape=jax.ShapeDtypeStruct(rhs.shape, BF16),
        in_specs=[VMEM] * 6,
        out_specs=ANY,
        scratch_shapes=[
            pltpu.VMEM((slabs, slots, nv, nb), BF16),
            index_scratch,
            pltpu.SemaphoreType.DMA((slabs,)),
        ],
        compiler_params=params(),
        name="finish",
    )(*(pin(x) for x in (shared, keep, send, rest, pair_keep, pair_send)))


def solution(mesh):
    in_specs = (
        P("stream", "span", None, None, None),
        P("stream", "span", None, None, None),
        P("stream", "span", None, None, None),
        P("stream", "span", None, None, None),
        P("stream", "span", None, None),
        P("stream", "span", None, None),
        P("stream"),
        P("stream", "span", None),
    )
    out_specs = P("stream", "span", None, None, None)
    return jax.shard_map(local, mesh=mesh, in_specs=in_specs, out_specs=out_specs, check_vma=False)
```

```python
import functools

import jax
import jax.numpy as jnp
from jax import lax
from jax.experimental import pallas as pl
from jax.experimental.pallas import tpu as pltpu
from jax.sharding import PartitionSpec as P

F32 = jnp.float32
BF16 = jnp.bfloat16
VMEM = pl.BlockSpec(memory_space=pltpu.VMEM)
SMEM = pl.BlockSpec(memory_space=pltpu.SMEM)
ANY = pl.BlockSpec(memory_space=pl.ANY)
STEP = 2_300_000_000
PAD = 16
JOINED = (4, 5)


def pin(x):
    return pltpu.with_memory_space_constraint(x, pltpu.VMEM)


def in_hbm(x):
    return pltpu.with_memory_space_constraint(x, pltpu.HBM)


def in_vmem(shape, dtype=BF16):
    return pltpu.VMEM(shape, dtype)


def params(mib=16):
    return pltpu.CompilerParams(vmem_limit_bytes=mib * 1024 * 1024)


def cost(flops, size):
    return pl.CostEstimate(flops=flops, bytes_accessed=size, transcendentals=0)


def dot(a, b, dims=((1,), (0,))):
    return lax.dot_general(a, b, (dims, ((), ())), preferred_element_type=F32)


def place():
    position = lax.axis_index("stream")
    return lax.rem(position, 2), lax.rem(lax.div(position, 2), 2), lax.div(position, 4)


def front_half(chip, group):
    return jnp.logical_and(chip == 0, group == JOINED[1])


def back_half(chip, group):
    return jnp.logical_and(chip == 1, group == JOINED[0])


def last_group(group):
    return group == lax.div(lax.axis_size("stream"), 4) - 1


def half_of(core, kept):
    return core if kept else 1 - core


def outer_kernel(prev, for_sent, for_kept, sem):
    core, _, _ = place()
    last = prev.shape[1] - 1
    copies = [pltpu.make_async_copy(prev.at[0, pl.ds(core * last, 1)], for_sent, sem.at[0]),
              pltpu.make_async_copy(prev.at[0, pl.ds((1 - core) * last, 1)], for_kept, sem.at[1])]
    for copy in copies:
        copy.start()
    for copy in copies:
        copy.wait()


def maps_of_half(upper_half, halo, hbm, out, edge, u, d, rhs, prev, lower, upper, index, u_sem, d_sem, sem):
    rhs_hbm, prev_hbm, u_hbm, d_hbm, lower_hbm, upper_hbm, index_hbm = hbm
    half, slots, nv, nb = rhs.shape
    first = upper_half * half
    step = nv + nb
    small = [
        pltpu.make_async_copy(index_hbm.at[0, pl.ds(first, half)], index, sem.at[0]),
        pltpu.make_async_copy(lower_hbm.at[0, pl.ds(first, half)], lower, sem.at[1]),
        pltpu.make_async_copy(upper_hbm.at[0, pl.ds(first, half)], upper, sem.at[2]),
        pltpu.make_async_copy(
            prev_hbm.at[0, pl.ds(upper_half * (half - 1), half + 1)], prev.at[pl.ds(1 - upper_half, half + 1)], sem.at[3]),
        pltpu.make_async_copy(rhs_hbm.at[0, pl.ds(first, half)], rhs, sem.at[4]),
    ]
    blocks = [(pltpu.make_async_copy(u_hbm.at[0, first + j], u.at[j], u_sem.at[j]),
               pltpu.make_async_copy(d_hbm.at[0, first + j], d.at[j], d_sem.at[j])) for j in range(half)]
    for copy in (*blocks[0], *small, *blocks[1]):
        copy.start()
    prev[upper_half * (half + 1)] = jnp.zeros((slots, nv, nb), BF16) if halo is None else halo[0]
    for copy in small:
        copy.wait()
    rows = lax.broadcasted_iota(jnp.int32, (PAD, nb), 0)
    for j in range(half):
        for copy in blocks[j]:
            copy.wait()
        tile = jnp.zeros((PAD, nb), F32)
        for k in range(slots):
            side = (lower[j, k : k + 1, :] * prev[j, k].astype(F32)
                    + upper[j, k : k + 1, :] * prev[j + 2, k].astype(F32))
            part = rhs[j, k].astype(F32) - side
            c = dot(part.astype(BF16), d[j, k], ((1,), (1,)))
            b = -dot(u[j, k], d[j, k], ((0,), (1,)))
            out[j, pl.ds(k * step, nv), :] = c.astype(BF16)
            out[j, pl.ds(k * step + nv, nb), :] = b.astype(BF16)
            tile = tile + jnp.where(rows == k, index[j, k].astype(F32), 0.0)
        out[j, pl.ds(slots * step, PAD), :] = tile.astype(BF16)
    if edge is None:
        return
    edge_d, edge_part, edge_gain = edge
    j = upper_half * (half - 1)
    edge_d[...] = d[j]
    edge_gain[...] = jnp.where(upper_half == 1, upper[j], lower[j])
    for k in range(slots):
        side = (lower[j, pl.ds(k, 1), :] * prev[j, k].astype(F32)
                + upper[j, pl.ds(k, 1), :] * prev[j + 2, k].astype(F32))
        edge_part[k] = rhs[j, k].astype(F32) - side


def sent_kernel(*refs):
    core, _, _ = place()
    maps_of_half(half_of(core, False), None, refs[:7], refs[7], refs[8:11], *refs[11:])


def kept_kernel(halo, *refs):
    core, _, _ = place()
    maps_of_half(half_of(core, True), halo, refs[:7], refs[7], None, *refs[8:])


def edge_kernel(halo, edge_d, edge_part, edge_gain, maps_in, maps):
    core, _, _ = place()
    slots, nv, nb = edge_part.shape
    j = half_of(core, False) * (maps.shape[0] - 1)
    for k in range(slots):
        part = edge_part[k] - edge_gain[pl.ds(k, 1), :] * halo[0, k].astype(F32)
        c = dot(part.astype(BF16), edge_d[k], ((1,), (1,)))
        maps[j, pl.ds(k * (nv + nb), nv), :] = c.astype(BF16)


def slot_scalars(tile, scratch, slots):
    scratch[...] = tile.astype(jnp.int32)
    return [scratch[k, 0] for k in range(slots)]


def compose(lo, hi, out, scratch, slots, nv, nb):
    step = nv + nb
    tile_lo = lo[pl.ds(slots * step, PAD), :].astype(F32)
    tile_hi = hi[pl.ds(slots * step, PAD), :].astype(F32)
    picks = slot_scalars(tile_hi, scratch, slots)
    tile = jnp.zeros_like(tile_hi)
    for n in range(slots):
        tile = tile + jnp.where(tile_hi == n, tile_lo[n : n + 1, :], 0.0)
    out[pl.ds(slots * step, PAD), :] = tile.astype(BF16)
    for k in range(slots):
        x = lo[pl.ds(pl.multiple_of(picks[k] * step, 16), step), :]
        y = dot(x, hi[pl.ds(k * step + nv, nb), :])
        c = hi[pl.ds(k * step, nv), :].astype(F32)
        out[pl.ds(k * step, nv), :] = (y[:nv] + c).astype(BF16)
        out[pl.ds(k * step + nv, nb), :] = y[nv:].astype(BF16)


def pair_kernel(slots, nv, keep, recv, out_keep, out_send, start, scratch):
    core, chip, _ = place()
    nb = keep.shape[-1]
    for here, lo, hi in ((0, keep, recv), (1, recv, keep)):
        @pl.when(core == here)
        def _():
            compose(lo.at[1 - chip], hi.at[1 - chip], out_send, scratch, slots, nv, nb)
            compose(lo.at[chip], hi.at[chip], out_keep, scratch, slots, nv, nb)
    for k in range(slots):
        start[chip, k] = out_keep[pl.ds(k * (nv + nb), nv), :]
        start[1 - chip, k] = out_send[pl.ds(k * (nv + nb), nv), :]


def apply_map(x, m, out, scratch, slots, nv, nb, active=None):
    step = nv + nb
    picks = slot_scalars(m[pl.ds(slots * step, PAD), :].astype(F32), scratch, slots)
    for k in range(slots):
        y = dot(x[picks[k]], m[pl.ds(k * step + nv, nb), :]) + m[pl.ds(k * step, nv), :].astype(F32)
        if active is not None:
            y = jnp.where(active[pl.ds(k, 1), :] > 0.0, y, 0.0)
        out[k] = y.astype(BF16)


def rest_kernel(slots, nv, widths, even, odd, out, active, scratch):
    core, _, _ = place()
    half, _, nb = out.shape
    active[...] = jnp.where(lax.broadcasted_iota(jnp.int32, (slots, nb), 0) < widths[0], 1.0, 0.0)

    @pl.when(core == 1)
    def _():
        for j in range(half):
            compose(even.at[j], odd.at[j], out.at[j], scratch, slots, nv, nb)


def first_kernel(slots, nv, arrived, keep, send, out_front, out_back, scratch):
    nb = keep.shape[-1]
    apply_map(arrived.at[0], send, out_front, scratch, slots, nv, nb)
    apply_map(arrived.at[1], keep, out_back, scratch, slots, nv, nb)


def second_kernel(slots, nv, front, back, keep, recv, state, inflow, middle, scratch):
    _, chip, _ = place()
    nb = keep.shape[-1]
    inflow[...] = front[...] + back[...]
    for here, lo, hi in ((0, keep, recv), (1, recv, keep)):
        @pl.when(chip == here)
        def _():
            apply_map(inflow, lo, middle, scratch, slots, nv, nb)
            apply_map(middle, hi, state, scratch, slots, nv, nb)


def group_kernel(slots, nv, keep, recv, out, scratch):
    _, chip, _ = place()
    nb = out.shape[-1]
    for here, lo, hi in ((0, keep, recv), (1, recv, keep)):
        @pl.when(chip == here)
        def _():
            compose(lo, hi, out, scratch, slots, nv, nb)


def join_kernel(slots, nv, group, recv, out, scratch):
    _, chip, number = place()
    nb = out.shape[-1]
    front, back = front_half(chip, number), back_half(chip, number)

    @pl.when(front)
    def _():
        compose(recv, group, out, scratch, slots, nv, nb)

    @pl.when(back)
    def _():
        compose(group, recv, out, scratch, slots, nv, nb)

    @pl.when(jnp.logical_not(jnp.logical_or(front, back)))
    def _():
        out[...] = group[...]


def hop_kernel(slots, nv, recv, chain, inflow, out, inflow_out, scratch):
    apply_map(recv, chain, out, scratch, slots, nv, chain.shape[-1])
    inflow_out[...] = inflow[...] + recv[...]


def fill_kernel(slots, nv, inflow, chain, group, out, scratch):
    _, chip, _ = place()
    for here, maps in ((0, chain), (1, group)):
        @pl.when(chip == here)
        def _():
            apply_map(inflow, maps, out, scratch, slots, nv, group.shape[-1])


def share_kernel(slots, nv, arrived, passed, filled, inflow, joined, before_last, keep, recv, out, total, middle, scratch):
    _, chip, number = place()
    nb = keep.shape[-1]
    total[...] = inflow[...] + arrived[...] + passed[...] + filled[...]

    for condition, maps in ((front_half(chip, number), joined), (last_group(number), before_last)):
        @pl.when(condition)
        def _():
            apply_map(total, maps, middle, scratch, slots, nv, nb)
            total[...] = middle[...]

    out[0] = total[...]
    for here, lo in ((0, keep), (1, recv)):
        @pl.when(chip == here)
        def _():
            apply_map(total, lo, out.at[1], scratch, slots, nv, nb)


def finish_kernel(slots, nv, active, shared, keep, send, rest, pair_keep, pair_send, out, result, scratch, sem):
    core, chip, _ = place()
    slabs, nb = out.shape[1], out.shape[-1]
    half = slabs // 2
    even = [(keep if m < half else send).at[m % half] for m in range(slabs)]
    odd = [rest.at[m] for m in range(half)]
    for condition, maps in (
        (core == 0, even),
        (jnp.logical_and(core == 1, chip == 0), [*odd, pair_keep, pair_send]),
        (jnp.logical_and(core == 1, chip == 1), [*odd, pair_send, pair_keep]),
    ):
        @pl.when(condition)
        def _():
            copies = []
            for m in range(slabs):
                x = shared.at[2 * (m % 2) + m // 2, chip]
                apply_map(x, maps[m], result.at[m], scratch.at[m], slots, nv, nb, active)
                copies.append(pltpu.make_async_copy(result.at[m], out.at[0, m], sem.at[m]))
                copies[-1].start()
            for copy in copies:
                copy.wait()


def local(rhs, previous, inverse_blocks, upstream_blocks, lower_gain, upper_gain, widths, upstream_index):
    _, slabs, slots, nv, nb = rhs.shape
    half = slabs // 2
    sections, peers = lax.axis_size("stream"), lax.axis_size("span")
    groups = sections // 4
    assert groups > JOINED[1] + 2
    rows = slots * (nv + nb) + PAD

    half_shape = in_vmem((half, rows, nb))
    one_shape = in_vmem((rows, nb))
    vec_shape = in_vmem((slots, nv, nb))
    edge_shape = in_vmem((1, slots, nv, nb))
    index_scratch = pltpu.VMEM((PAD, nb), jnp.int32)
    block_shape, gain_shape = (half, slots, nb, nb), (half, slots, nb)

    for_sent, for_kept = pl.pallas_call(
        outer_kernel,
        out_shape=(edge_shape, edge_shape),
        in_specs=[ANY],
        out_specs=(VMEM, VMEM),
        scratch_shapes=[pltpu.SemaphoreType.DMA((2,))],
        compiler_params=params(),
        name="outer_slabs",
    )(in_hbm(previous))

    def beside(x, kept):
        pairs = []
        for i in range(sections):
            for s in range(peers - 1):
                here, above = i * peers + s, i * peers + s + 1
                pairs.append((above, here) if half_of(i % 2, kept) == 1 else (here, above))
        return lax.ppermute(x, ("stream", "span"), pairs)

    operands = [in_hbm(x) for x in (
        rhs, previous, upstream_blocks, inverse_blocks, lower_gain, upper_gain, upstream_index)]
    maps_scratch = [
        pltpu.VMEM(block_shape, BF16),
        pltpu.VMEM(block_shape, BF16),
        pltpu.VMEM((half, slots, nv, nb), BF16),
        pltpu.VMEM((half + 2, slots, nv, nb), BF16),
        pltpu.VMEM(gain_shape, F32),
        pltpu.VMEM(gain_shape, F32),
        pltpu.SMEM((half, slots), jnp.int32),
        pltpu.SemaphoreType.DMA((half,)),
        pltpu.SemaphoreType.DMA((half,)),
        pltpu.SemaphoreType.DMA((5,)),
    ]
    halo_sent, halo_kept = beside(for_sent, False), beside(for_kept, True)
    send, *edge = pl.pallas_call(
        sent_kernel,
        out_shape=(half_shape, in_vmem((slots, nb, nb)), in_vmem((slots, nv, nb), F32), in_vmem((slots, nb), F32)),
        in_specs=[ANY] * 7,
        out_specs=(VMEM,) * 4,
        scratch_shapes=maps_scratch,
        compiler_params=params(),
        cost_estimate=cost(STEP, 0),
        name="maps_sent",
    )(*operands)
    send = pl.pallas_call(
        edge_kernel,
        out_shape=half_shape,
        in_specs=[VMEM] * 5,
        out_specs=VMEM,
        input_output_aliases={4: 0},
        compiler_params=params(),
        name="edge_sent",
    )(*(pin(x) for x in (halo_sent, *edge, send)))
    keep = pl.pallas_call(
        kept_kernel,
        out_shape=half_shape,
        in_specs=[VMEM] + [ANY] * 7,
        out_specs=VMEM,
        scratch_shapes=maps_scratch,
        compiler_params=params(),
        cost_estimate=cost(10 * STEP, 0),
        name="maps_kept",
    )(pin(halo_kept), *operands)

    def call(kernel, outs, name, *args, scratch=(), flops=0):
        return pl.pallas_call(
            functools.partial(kernel, slots, nv),
            out_shape=outs,
            in_specs=[VMEM] * len(args),
            out_specs=(VMEM,) * len(outs) if isinstance(outs, tuple) else VMEM,
            scratch_shapes=[*scratch, index_scratch],
            compiler_params=params(),
            cost_estimate=cost(flops, 0) if flops else None,
            name=name,
        )(*(pin(x) for x in args))

    def stream(x, *hops):
        pairs = []
        for chip, source, target in hops:
            pairs += [(4 * source + 2 * chip + core, 4 * target + 2 * chip + core) for core in range(2)]
        return lax.ppermute(x, "stream", pairs)

    recv = lax.ppermute(send, "stream", [(i, i ^ 1) for i in range(sections)])
    pair_keep, pair_send, pair_start = call(
        pair_kernel, (one_shape, one_shape, in_vmem((2, slots, nv, nb))), "compose_chip", keep, recv)

    arrived = lax.ppermute(pair_start, "stream", [(0, 2), (1, 3)])
    recv_second = lax.ppermute(pair_send, "stream", [(i, i ^ 2) for i in range(4, 8)])
    recv_later = lax.ppermute(pair_send, "stream", [(i, i ^ 2) for i in range(8, sections)])
    front, back = call(first_kernel, (vec_shape, vec_shape), "first_group", arrived, pair_keep, pair_send, flops=STEP)
    back = lax.ppermute(back, "stream", [(2, 6), (3, 7)])
    front = lax.ppermute(front, "stream", [(2, 4), (3, 5)])
    state, inflow = call(
        second_kernel, (vec_shape, vec_shape), "second_group", front, back, pair_keep, recv_second, scratch=(vec_shape,), flops=STEP)
    arrived = stream(state, (0, 1, 2), (1, 1, 2))
    group = call(group_kernel, one_shape, "compose_group", pair_keep, recv_later, flops=STEP)

    keep_again, pair_send_again, state = lax.optimization_barrier((keep, pair_send, state))
    recv_first = lax.ppermute(pair_send_again, "stream", [(i, i ^ 2) for i in range(4)])
    even = lax.ppermute(keep_again, "stream", [(i, i + 1) for i in range(0, sections, 2)])
    rest, active = pl.pallas_call(
        functools.partial(rest_kernel, slots, nv),
        out_shape=(half_shape, in_vmem((slots, nb), F32)),
        in_specs=[SMEM, VMEM, VMEM],
        out_specs=(VMEM, VMEM),
        scratch_shapes=[index_scratch],
        compiler_params=params(),
        cost_estimate=cost(STEP, 0),
        name="compose_rest",
    )(widths, pin(even), pin(send))

    a, b = JOINED
    last = groups - 1
    join_recv = stream(group, (0, a, b), (1, b, a))
    last_recv = stream(group, (0, last - 1, last), (1, last - 1, last))
    chain = call(join_kernel, one_shape, "compose_join", group, join_recv)
    chain, rest = lax.optimization_barrier((chain, rest))
    steps = [(2, 2), *((g, g) for g in range(3, a)), (b, a), *((g, g) for g in range(b + 1, last - 1))]
    for step, (front, back) in enumerate(steps):
        maps = group if front < a else chain
        state, inflow = call(hop_kernel, (vec_shape, vec_shape), "hop", arrived, maps, inflow, flops=STEP)
        if step + 1 < len(steps):
            arrived = stream(state, (0, front, steps[step + 1][0]), (1, back, steps[step + 1][1]))
        else:
            arrived = stream(state, (0, front, last), (1, back, last))
            passed = stream(state, (0, front, last - 1), (1, back, last - 1))
    filled = stream(call(fill_kernel, vec_shape, "fill", inflow, chain, group), (0, a - 1, a), (1, a, b))

    shares = call(
        share_kernel, in_vmem((2, slots, nv, nb)), "share",
        arrived, passed, filled, inflow, join_recv, last_recv, pair_keep, recv_first + recv_second + recv_later,
        scratch=(vec_shape, vec_shape))
    shared = lax.all_gather(
        shares, "stream", axis_index_groups=[[4 * g + r for r in range(4)] for g in range(groups)]
    )
    return pl.pallas_call(
        functools.partial(finish_kernel, slots, nv),
        out_shape=jax.ShapeDtypeStruct(rhs.shape, BF16),
        in_specs=[VMEM] * 7,
        out_specs=ANY,
        scratch_shapes=[
            pltpu.VMEM((slabs, slots, nv, nb), BF16),
            pltpu.VMEM((slabs, PAD, nb), jnp.int32),
            pltpu.SemaphoreType.DMA((slabs,)),
        ],
        compiler_params=params(),
        name="finish",
    )(*(pin(x) for x in (active, shared, keep, send, rest, pair_keep, pair_send)))


def solution(mesh):
    in_specs = (
        P("stream", "span", None, None, None),
        P("stream", "span", None, None, None),
        P("stream", "span", None, None, None),
        P("stream", "span", None, None, None),
        P("stream", "span", None, None),
        P("stream", "span", None, None),
        P("stream"),
        P("stream", "span", None),
    )
    out_specs = P("stream", "span", None, None, None)
    return jax.shard_map(local, mesh=mesh, in_specs=in_specs, out_specs=out_specs, check_vma=False)
```

```python
import functools

import jax
import jax.numpy as jnp
from jax import lax
from jax.experimental import pallas as pl
from jax.experimental.pallas import tpu as pltpu
from jax.sharding import PartitionSpec as P

F32 = jnp.float32
BF16 = jnp.bfloat16
VMEM = pl.BlockSpec(memory_space=pltpu.VMEM)
SMEM = pl.BlockSpec(memory_space=pltpu.SMEM)
ANY = pl.BlockSpec(memory_space=pl.ANY)
MICRO = 1_150_000_000
PAD = 16
JOINED = (4, 5)


def pin(x):
    return pltpu.with_memory_space_constraint(x, pltpu.VMEM)


def in_hbm(x):
    return pltpu.with_memory_space_constraint(x, pltpu.HBM)


def in_vmem(shape, dtype=BF16):
    return pltpu.VMEM(shape, dtype)


def params(mib=16):
    return pltpu.CompilerParams(vmem_limit_bytes=mib * 1024 * 1024)


def cost(flops, size):
    return pl.CostEstimate(flops=flops, bytes_accessed=size, transcendentals=0)


def dot(a, b, dims=((1,), (0,))):
    return lax.dot_general(a, b, (dims, ((), ())), preferred_element_type=F32)


def place():
    position = lax.axis_index("stream")
    return lax.rem(position, 2), lax.rem(lax.div(position, 2), 2), lax.div(position, 4)


def front_half(chip, group):
    return jnp.logical_and(chip == 0, group == JOINED[1])


def back_half(chip, group):
    return jnp.logical_and(chip == 1, group == JOINED[0])


def last_group(group):
    return group == lax.div(lax.axis_size("stream"), 4) - 1


def half_of(core, kept):
    return core if kept else 1 - core


def outer_kernel(prev, for_sent, for_kept, sem):
    core, _, _ = place()
    last = prev.shape[1] - 1
    copies = [pltpu.make_async_copy(prev.at[0, pl.ds(core * last, 1)], for_sent, sem.at[0]),
              pltpu.make_async_copy(prev.at[0, pl.ds((1 - core) * last, 1)], for_kept, sem.at[1])]
    for copy in copies:
        copy.start()
    for copy in copies:
        copy.wait()


def maps_of_half(upper_half, halo, hbm, out, edge, u, d, rhs, prev, lower, upper, index, u_sem, d_sem, sem):
    rhs_hbm, prev_hbm, u_hbm, d_hbm, lower_hbm, upper_hbm, index_hbm = hbm
    half, slots, nv, nb = rhs.shape
    first = upper_half * half
    step = nv + nb
    small = [
        pltpu.make_async_copy(index_hbm.at[0, pl.ds(first, half)], index, sem.at[0]),
        pltpu.make_async_copy(lower_hbm.at[0, pl.ds(first, half)], lower, sem.at[1]),
        pltpu.make_async_copy(upper_hbm.at[0, pl.ds(first, half)], upper, sem.at[2]),
        pltpu.make_async_copy(
            prev_hbm.at[0, pl.ds(upper_half * (half - 1), half + 1)], prev.at[pl.ds(1 - upper_half, half + 1)], sem.at[3]),
        pltpu.make_async_copy(rhs_hbm.at[0, pl.ds(first, half)], rhs, sem.at[4]),
    ]
    blocks = [(pltpu.make_async_copy(u_hbm.at[0, first + j], u.at[j], u_sem.at[j]),
               pltpu.make_async_copy(d_hbm.at[0, first + j], d.at[j], d_sem.at[j])) for j in range(half)]
    for copy in (*blocks[0], *small, *blocks[1]):
        copy.start()
    prev[upper_half * (half + 1)] = jnp.zeros((slots, nv, nb), BF16) if halo is None else halo[0]
    for copy in small:
        copy.wait()
    rows = lax.broadcasted_iota(jnp.int32, (PAD, nb), 0)
    for j in range(half):
        for copy in blocks[j]:
            copy.wait()
        tile = jnp.zeros((PAD, nb), F32)
        for k in range(slots):
            side = (lower[j, k : k + 1, :] * prev[j, k].astype(F32)
                    + upper[j, k : k + 1, :] * prev[j + 2, k].astype(F32))
            part = rhs[j, k].astype(F32) - side
            c = dot(part.astype(BF16), d[j, k], ((1,), (1,)))
            b = -dot(u[j, k], d[j, k], ((0,), (1,)))
            out[j, pl.ds(k * step, nv), :] = c.astype(BF16)
            out[j, pl.ds(k * step + nv, nb), :] = b.astype(BF16)
            tile = tile + jnp.where(rows == k, index[j, k].astype(F32), 0.0)
        out[j, pl.ds(slots * step, PAD), :] = tile.astype(BF16)
    if edge is None:
        return
    edge_d, edge_part, edge_gain = edge
    j = upper_half * (half - 1)
    edge_d[...] = d[j]
    edge_gain[...] = jnp.where(upper_half == 1, upper[j], lower[j])
    for k in range(slots):
        side = (lower[j, pl.ds(k, 1), :] * prev[j, k].astype(F32)
                + upper[j, pl.ds(k, 1), :] * prev[j + 2, k].astype(F32))
        edge_part[k] = rhs[j, k].astype(F32) - side


def sent_kernel(*refs):
    core, _, _ = place()
    maps_of_half(half_of(core, False), None, refs[:7], refs[7], refs[8:11], *refs[11:])


def kept_kernel(halo, *refs):
    core, _, _ = place()
    maps_of_half(half_of(core, True), halo, refs[:7], refs[7], None, *refs[8:])


def edge_kernel(halo, edge_d, edge_part, edge_gain, maps_in, maps):
    core, _, _ = place()
    slots, nv, nb = edge_part.shape
    j = half_of(core, False) * (maps.shape[0] - 1)
    for k in range(slots):
        part = edge_part[k] - edge_gain[pl.ds(k, 1), :] * halo[0, k].astype(F32)
        c = dot(part.astype(BF16), edge_d[k], ((1,), (1,)))
        maps[j, pl.ds(k * (nv + nb), nv), :] = c.astype(BF16)


def slot_scalars(tile, scratch, slots):
    scratch[...] = tile.astype(jnp.int32)
    return [scratch[k, 0] for k in range(slots)]


def compose(lo, hi, out, scratch, slots, nv, nb):
    step = nv + nb
    tile_lo = lo[pl.ds(slots * step, PAD), :].astype(F32)
    tile_hi = hi[pl.ds(slots * step, PAD), :].astype(F32)
    picks = slot_scalars(tile_hi, scratch, slots)
    tile = jnp.zeros_like(tile_hi)
    for n in range(slots):
        tile = tile + jnp.where(tile_hi == n, tile_lo[n : n + 1, :], 0.0)
    out[pl.ds(slots * step, PAD), :] = tile.astype(BF16)
    for k in range(slots):
        x = lo[pl.ds(pl.multiple_of(picks[k] * step, 16), step), :]
        y = dot(x, hi[pl.ds(k * step + nv, nb), :])
        c = hi[pl.ds(k * step, nv), :].astype(F32)
        out[pl.ds(k * step, nv), :] = (y[:nv] + c).astype(BF16)
        out[pl.ds(k * step + nv, nb), :] = y[nv:].astype(BF16)


def pair_kernel(slots, nv, keep, recv, out_keep, out_send, start, scratch):
    core, chip, _ = place()
    nb = keep.shape[-1]
    for here, lo, hi in ((0, keep, recv), (1, recv, keep)):
        @pl.when(core == here)
        def _():
            compose(lo.at[1 - chip], hi.at[1 - chip], out_send, scratch, slots, nv, nb)
            compose(lo.at[chip], hi.at[chip], out_keep, scratch, slots, nv, nb)
    for k in range(slots):
        start[chip, k] = out_keep[pl.ds(k * (nv + nb), nv), :]
        start[1 - chip, k] = out_send[pl.ds(k * (nv + nb), nv), :]


def picks_of(m, scratch, slots, step):
    return slot_scalars(m[pl.ds(slots * step, PAD), :].astype(F32), scratch, slots)


def apply_map(x, m, out, scratch, slots, nv, nb, active=None, picks=None):
    step = nv + nb
    if picks is None:
        picks = picks_of(m, scratch, slots, step)
    for k in range(slots):
        y = dot(x[picks[k]], m[pl.ds(k * step + nv, nb), :]) + m[pl.ds(k * step, nv), :].astype(F32)
        if active is not None:
            y = jnp.where(active[pl.ds(k, 1), :] > 0.0, y, 0.0)
        out[k] = y.astype(BF16)


def rest_kernel(slots, nv, widths, even, odd, out, active, scratch):
    core, _, _ = place()
    half, _, nb = out.shape
    active[...] = jnp.where(lax.broadcasted_iota(jnp.int32, (slots, nb), 0) < widths[0], 1.0, 0.0)

    @pl.when(core == 1)
    def _():
        for j in range(half):
            compose(even.at[j], odd.at[j], out.at[j], scratch, slots, nv, nb)


def first_kernel(slots, nv, arrived, keep, send, out_front, out_back, scratch):
    nb = keep.shape[-1]
    apply_map(arrived.at[0], send, out_front, scratch, slots, nv, nb)
    apply_map(arrived.at[1], keep, out_back, scratch, slots, nv, nb)


def second_kernel(slots, nv, front, back, keep, recv, state, inflow, middle, scratch):
    _, chip, _ = place()
    nb = keep.shape[-1]
    inflow[...] = front[...] + back[...]
    for here, lo, hi in ((0, keep, recv), (1, recv, keep)):
        @pl.when(chip == here)
        def _():
            apply_map(inflow, lo, middle, scratch, slots, nv, nb)
            apply_map(middle, hi, state, scratch, slots, nv, nb)


def group_kernel(slots, nv, keep, recv, out, scratch):
    _, chip, _ = place()
    nb = out.shape[-1]
    for here, lo, hi in ((0, keep, recv), (1, recv, keep)):
        @pl.when(chip == here)
        def _():
            compose(lo, hi, out, scratch, slots, nv, nb)


def join_kernel(slots, nv, group, recv, out, scratch):
    _, chip, number = place()
    nb = out.shape[-1]
    front, back = front_half(chip, number), back_half(chip, number)

    @pl.when(front)
    def _():
        compose(recv, group, out, scratch, slots, nv, nb)

    @pl.when(back)
    def _():
        compose(group, recv, out, scratch, slots, nv, nb)

    @pl.when(jnp.logical_not(jnp.logical_or(front, back)))
    def _():
        out[...] = group[...]


def hop_kernel(slots, nv, recv, chain, inflow, out, inflow_out, scratch):
    apply_map(recv, chain, out, scratch, slots, nv, chain.shape[-1])
    inflow_out[...] = inflow[...] + recv[...]


def fill_kernel(slots, nv, inflow, chain, group, out, scratch):
    _, chip, _ = place()
    for here, maps in ((0, chain), (1, group)):
        @pl.when(chip == here)
        def _():
            apply_map(inflow, maps, out, scratch, slots, nv, group.shape[-1])


def share_kernel(slots, nv, arrived, passed, filled, inflow, joined, before_last, keep, recv, out, total, middle, scratch):
    _, chip, number = place()
    nb = keep.shape[-1]
    total[...] = inflow[...] + arrived[...] + passed[...] + filled[...]

    for condition, maps in ((front_half(chip, number), joined), (last_group(number), before_last)):
        @pl.when(condition)
        def _():
            apply_map(total, maps, middle, scratch, slots, nv, nb)
            total[...] = middle[...]

    out[0] = total[...]
    for here, lo in ((0, keep), (1, recv)):
        @pl.when(chip == here)
        def _():
            apply_map(total, lo, out.at[1], scratch, slots, nv, nb)


def finish_kernel(slots, nv, active, shared, keep, send, rest, pair_keep, pair_send, out, result, scratch, sem):
    core, chip, _ = place()
    slabs, nb = out.shape[1], out.shape[-1]
    half = slabs // 2
    even = [(keep if m < half else send).at[m % half] for m in range(slabs)]
    odd = [rest.at[m] for m in range(half)]
    for condition, maps in (
        (core == 0, even),
        (jnp.logical_and(core == 1, chip == 0), [*odd, pair_keep, pair_send]),
        (jnp.logical_and(core == 1, chip == 1), [*odd, pair_send, pair_keep]),
    ):
        @pl.when(condition)
        def _():
            copies = []
            picks = [picks_of(maps[m], scratch.at[m], slots, nv + nb) for m in range(slabs)]
            for m in range(slabs):
                x = shared.at[2 * (m % 2) + m // 2, chip]
                apply_map(x, maps[m], result.at[m], None, slots, nv, nb, active, picks[m])
                copies.append(pltpu.make_async_copy(result.at[m], out.at[0, m], sem.at[m]))
                copies[-1].start()
            for copy in copies:
                copy.wait()


def local(rhs, previous, inverse_blocks, upstream_blocks, lower_gain, upper_gain, widths, upstream_index):
    _, slabs, slots, nv, nb = rhs.shape
    half = slabs // 2
    sections, peers = lax.axis_size("stream"), lax.axis_size("span")
    groups = sections // 4
    assert groups > JOINED[1] + 2
    rows = slots * (nv + nb) + PAD

    half_shape = in_vmem((half, rows, nb))
    one_shape = in_vmem((rows, nb))
    vec_shape = in_vmem((slots, nv, nb))
    edge_shape = in_vmem((1, slots, nv, nb))
    index_scratch = pltpu.VMEM((PAD, nb), jnp.int32)
    block_shape, gain_shape = (half, slots, nb, nb), (half, slots, nb)

    for_sent, for_kept = pl.pallas_call(
        outer_kernel,
        out_shape=(edge_shape, edge_shape),
        in_specs=[ANY],
        out_specs=(VMEM, VMEM),
        scratch_shapes=[pltpu.SemaphoreType.DMA((2,))],
        compiler_params=params(),
        name="outer_slabs",
    )(in_hbm(previous))

    def beside(x, kept):
        pairs = []
        for i in range(sections):
            for s in range(peers - 1):
                here, above = i * peers + s, i * peers + s + 1
                pairs.append((above, here) if half_of(i % 2, kept) == 1 else (here, above))
        return lax.ppermute(x, ("stream", "span"), pairs)

    operands = [in_hbm(x) for x in (
        rhs, previous, upstream_blocks, inverse_blocks, lower_gain, upper_gain, upstream_index)]
    maps_scratch = [
        pltpu.VMEM(block_shape, BF16),
        pltpu.VMEM(block_shape, BF16),
        pltpu.VMEM((half, slots, nv, nb), BF16),
        pltpu.VMEM((half + 2, slots, nv, nb), BF16),
        pltpu.VMEM(gain_shape, F32),
        pltpu.VMEM(gain_shape, F32),
        pltpu.SMEM((half, slots), jnp.int32),
        pltpu.SemaphoreType.DMA((half,)),
        pltpu.SemaphoreType.DMA((half,)),
        pltpu.SemaphoreType.DMA((5,)),
    ]
    halo_sent, halo_kept = beside(for_sent, False), beside(for_kept, True)
    send, *edge = pl.pallas_call(
        sent_kernel,
        out_shape=(half_shape, in_vmem((slots, nb, nb)), in_vmem((slots, nv, nb), F32), in_vmem((slots, nb), F32)),
        in_specs=[ANY] * 7,
        out_specs=(VMEM,) * 4,
        scratch_shapes=maps_scratch,
        compiler_params=params(),
        cost_estimate=cost(2 * MICRO, 0),
        name="maps_sent",
    )(*operands)
    send = pl.pallas_call(
        edge_kernel,
        out_shape=half_shape,
        in_specs=[VMEM] * 5,
        out_specs=VMEM,
        input_output_aliases={4: 0},
        compiler_params=params(),
        name="edge_sent",
    )(*(pin(x) for x in (halo_sent, *edge, send)))
    keep = pl.pallas_call(
        kept_kernel,
        out_shape=half_shape,
        in_specs=[VMEM] + [ANY] * 7,
        out_specs=VMEM,
        scratch_shapes=maps_scratch,
        compiler_params=params(),
        cost_estimate=cost(20 * MICRO, 0),
        name="maps_kept",
    )(pin(halo_kept), *operands)

    def call(kernel, outs, name, *args, scratch=(), flops=0):
        return pl.pallas_call(
            functools.partial(kernel, slots, nv),
            out_shape=outs,
            in_specs=[VMEM] * len(args),
            out_specs=(VMEM,) * len(outs) if isinstance(outs, tuple) else VMEM,
            scratch_shapes=[*scratch, index_scratch],
            compiler_params=params(),
            cost_estimate=cost(flops, 0) if flops else None,
            name=name,
        )(*(pin(x) for x in args))

    def stream(x, *hops):
        pairs = []
        for chip, source, target in hops:
            pairs += [(4 * source + 2 * chip + core, 4 * target + 2 * chip + core) for core in range(2)]
        return lax.ppermute(x, "stream", pairs)

    recv = lax.ppermute(send, "stream", [(i, i ^ 1) for i in range(sections)])
    pair_keep, pair_send, pair_start = call(
        pair_kernel, (one_shape, one_shape, in_vmem((2, slots, nv, nb))), "compose_chip", keep, recv)

    arrived = lax.ppermute(pair_start, "stream", [(0, 2), (1, 3)])
    recv_second = lax.ppermute(pair_send, "stream", [(i, i ^ 2) for i in range(4, 8)])
    recv_later = lax.ppermute(pair_send, "stream", [(i, i ^ 2) for i in range(8, sections)])
    front, back = call(first_kernel, (vec_shape, vec_shape), "first_group", arrived, pair_keep, pair_send, flops=MICRO)
    back = lax.ppermute(back, "stream", [(2, 6), (3, 7)])
    front = lax.ppermute(front, "stream", [(2, 4), (3, 5)])
    state, inflow = call(
        second_kernel, (vec_shape, vec_shape), "second_group", front, back, pair_keep, recv_second, scratch=(vec_shape,), flops=2 * MICRO)
    arrived = stream(state, (0, 1, 2), (1, 1, 2))
    group = call(group_kernel, one_shape, "compose_group", pair_keep, recv_later, flops=4 * MICRO)

    keep_again, pair_send_again, state = lax.optimization_barrier((keep, pair_send, state))
    recv_first = lax.ppermute(pair_send_again, "stream", [(i, i ^ 2) for i in range(4)])
    even = lax.ppermute(keep_again, "stream", [(i, i + 1) for i in range(0, sections, 2)])
    rest, active = pl.pallas_call(
        functools.partial(rest_kernel, slots, nv),
        out_shape=(half_shape, in_vmem((slots, nb), F32)),
        in_specs=[SMEM, VMEM, VMEM],
        out_specs=(VMEM, VMEM),
        scratch_shapes=[index_scratch],
        compiler_params=params(),
        cost_estimate=cost(MICRO, 0),
        name="compose_rest",
    )(widths, pin(even), pin(send))

    a, b = JOINED
    last = groups - 1
    join_recv = stream(group, (0, a, b), (1, b, a))
    last_recv = stream(group, (0, last - 1, last), (1, last - 1, last))
    chain = call(join_kernel, one_shape, "compose_join", group, join_recv)
    steps = [(2, 2), *((g, g) for g in range(3, a)), (b, a), *((g, g) for g in range(b + 1, last - 1))]
    for step, (front, back) in enumerate(steps):
        maps = group if front < a else chain
        if step == 1:
            rest, arrived = lax.optimization_barrier((rest, arrived))
        state, inflow = call(hop_kernel, (vec_shape, vec_shape), "hop", arrived, maps, inflow, flops=3 * MICRO)
        if step + 1 < len(steps):
            arrived = stream(state, (0, front, steps[step + 1][0]), (1, back, steps[step + 1][1]))
        else:
            arrived = stream(state, (0, front, last), (1, back, last))
            passed = stream(state, (0, front, last - 1), (1, back, last - 1))
    filled = stream(call(fill_kernel, vec_shape, "fill", inflow, chain, group), (0, a - 1, a), (1, a, b))

    shares = call(
        share_kernel, in_vmem((2, slots, nv, nb)), "share",
        arrived, passed, filled, inflow, join_recv, last_recv, pair_keep, recv_first + recv_second + recv_later,
        scratch=(vec_shape, vec_shape))
    shared = lax.all_gather(
        shares, "stream", axis_index_groups=[[4 * g + r for r in range(4)] for g in range(groups)]
    )
    return pl.pallas_call(
        functools.partial(finish_kernel, slots, nv),
        out_shape=jax.ShapeDtypeStruct(rhs.shape, BF16),
        in_specs=[VMEM] * 7,
        out_specs=ANY,
        scratch_shapes=[
            pltpu.VMEM((slabs, slots, nv, nb), BF16),
            pltpu.VMEM((slabs, PAD, nb), jnp.int32),
            pltpu.SemaphoreType.DMA((slabs,)),
        ],
        compiler_params=params(),
        name="finish",
    )(*(pin(x) for x in (active, shared, keep, send, rest, pair_keep, pair_send)))


def solution(mesh):
    in_specs = (
        P("stream", "span", None, None, None),
        P("stream", "span", None, None, None),
        P("stream", "span", None, None, None),
        P("stream", "span", None, None, None),
        P("stream", "span", None, None),
        P("stream", "span", None, None),
        P("stream"),
        P("stream", "span", None),
    )
    out_specs = P("stream", "span", None, None, None)
    return jax.shard_map(local, mesh=mesh, in_specs=in_specs, out_specs=out_specs, check_vma=False)
```
